32 devices in a mesh: radial: 8 (over y, x, core), axial: 4 (over z).
Axes of the slice: x: 2, y: 2, z: 4, core: 2. Of those that a mesh axis runs over, the one named last changes fastest.
Arguments:
- rhs: float32 [2, 2, 96, 64, 512], P(None, None, None, 'radial', 'axial'), may hold values from -6 to 6
- mat_ids: int32 [96, 64, 512], P(None, 'radial', 'axial'), may hold values from 0 to 3
- stiff_table: float32 [4], replicated, may hold values from 0.5 to 4
- dens_table: float32 [4], replicated, may hold values from 0.5 to 2
- mass_shift: float32 [2], replicated, may hold values from 0.5 to 2
- harmonic: int32 [2], replicated, may hold values from 1 to 12
- radial_factor: float32 [2, 2, 16, 16], replicated, may hold values from -0.09375 to 0.09375
- axial_factor: float32 [2, 2, 64, 64], replicated, may hold values from -0.046875 to 0.046875
Outputs:
- solution: float32 [2, 2, 96, 64, 512], P(None, None, None, 'radial', 'axial')
- residual: float32 [2, 2, 96, 64, 512], P(None, None, None, 'radial', 'axial')
The draws below stay inside these ranges and needn't reach their ends.
All inputs are finite; a program needn't handle non-finite values.
Results may differ from the reference program's by a relative error of at most 0.00021.
Values sent between devices are 32-bit elements; how exact they have to be, the bound alone decides.
A program may use at most 128 MiB of HBM per device.

```python
import math
import jax
import jax.numpy as jnp
from jax import lax

CT = 96
HARM = 2
ITERS = 3
NSECT = 24
NMAT = 4
AR = 4
AA = 8
NR = 64
NA = 512
GR = 16
GA = 64


def touch_ends(values, stream_key, low, top_value):
    longest = values.shape.index(max(values.shape))
    spots = []
    for shift in (0, 1):
        where = [jax.random.randint(jax.random.fold_in(stream_key, axis), (), 0, length) for axis, length in enumerate(values.shape)]
        where[longest] = (where[longest] + shift) % values.shape[longest]
        spots.append(tuple(where))
    return values.at[spots[0]].set(low).at[spots[1]].set(top_value)


def steps_of(rng, shape, cuts, low, largest):
    def one(position, blocks):
        steps = jax.random.uniform(jax.random.fold_in(jax.random.fold_in(rng, 6), position), (blocks,), jnp.float32, low / len(cuts), largest / len(cuts))
        return jnp.repeat(jnp.exp(steps), shape[position] // blocks).reshape((-1,) + (1,) * (len(shape) - position - 1))

    level = one(*cuts[0])
    for cut in cuts[1:]:
        level = level * one(*cut)
    return level


def normal_values(rng, shape, scale, reach, pieces=(), kind=jnp.bfloat16):
    gain = steps_of(rng, shape, pieces, -0.22, 0.18) if pieces else 1.0
    entries = jax.random.normal(rng, shape, jnp.float32) * scale * gain
    return jnp.minimum(jnp.maximum(entries, -reach), reach).astype(kind)


def setup_inputs(seed: int = 0) -> dict:
    splits = jax.random.split(jax.random.key(seed), 9)
    rhs = normal_values(splits[0], (2, HARM, CT, NR, NA), 1.0, 6.0, ((3, 8), (4, 4)), jnp.float32)
    mat_ids = touch_ends(jax.random.randint(splits[1], (CT, NR, NA), 0, NMAT), jax.random.fold_in(splits[1], 1), 0, NMAT - 1).astype(jnp.int32)
    stiff_table = jnp.clip(jnp.exp(jax.random.uniform(splits[2], (NMAT,), jnp.float32, math.log(0.5), math.log(4.0))), 0.5, 4.0)
    dens_table = jnp.clip(jnp.exp(jax.random.uniform(splits[3], (NMAT,), jnp.float32, math.log(0.5), math.log(2.0))), 0.5, 2.0)
    mass_shift = jnp.clip(jax.random.uniform(splits[4], (HARM,), jnp.float32, 0.5, 2.0), 0.5, 2.0)
    harmonic = jax.random.randint(splits[5], (HARM,), 1, NSECT // 2 + 1).astype(jnp.int32)
    radial_factor = normal_values(splits[6], (2, HARM, GR, GR), (256 * GR) ** -0.5, 0.09375, (), jnp.float32)
    axial_factor = normal_values(splits[7], (2, HARM, GA, GA), (256 * GA) ** -0.5, 0.046875, (), jnp.float32)
    return {"rhs": rhs, "mat_ids": mat_ids, "stiff_table": stiff_table, "dens_table": dens_table, "mass_shift": mass_shift, "harmonic": harmonic, "radial_factor": radial_factor, "axial_factor": axial_factor}


LOSS_FACTOR = 0.2
RELAXATION = 0.6


def material(mat_ids, table):
    result = jnp.zeros(mat_ids.shape, table.dtype)
    for entry in range(table.shape[0]):
        result = result + jnp.where(mat_ids == entry, table[entry], jnp.zeros((), table.dtype))
    return result


def couplings(stiffness, padded):
    return (0.5 * (stiffness + padded[:, 2:, 1:-1]),
            0.5 * (stiffness + padded[:, :-2, 1:-1]),
            0.5 * (stiffness + padded[:, 1:-1, 2:]),
            0.5 * (stiffness + padded[:, 1:-1, :-2]),
            0.5 * (stiffness + jnp.roll(stiffness, -1, 0)),
            0.5 * (stiffness + jnp.roll(stiffness, 1, 0)))


def neighbours(values, padded, weights, cosines, sines):
    summed = weights[0] * padded[:, :, :, 2:, 1:-1] + weights[1] * padded[:, :, :, :-2, 1:-1]
    summed = summed + weights[2] * padded[:, :, :, 1:-1, 2:] + weights[3] * padded[:, :, :, 1:-1, :-2]
    real_part = values[0]
    imag_part = values[1]
    cosine = cosines[:, None, None, None]
    sine = sines[:, None, None, None]
    wrap_real = cosine * real_part[:, :1] - sine * imag_part[:, :1]
    wrap_imag = sine * real_part[:, :1] + cosine * imag_part[:, :1]
    ahead = jnp.stack([jnp.concatenate([real_part[:, 1:], wrap_real], 1),
                       jnp.concatenate([imag_part[:, 1:], wrap_imag], 1)])
    back_real = cosine * real_part[:, -1:] + sine * imag_part[:, -1:]
    back_imag = cosine * imag_part[:, -1:] - sine * real_part[:, -1:]
    behind = jnp.stack([jnp.concatenate([back_real, real_part[:, :-1]], 1),
                        jnp.concatenate([back_imag, imag_part[:, :-1]], 1)])
    return summed + weights[4] * ahead + weights[5] * behind


def operate(values, padded, weights, diag_real, diag_imag, cosines, sines):
    coupled = neighbours(values, padded, weights, cosines, sines)
    real_out = diag_real * values[0] - diag_imag * values[1] - (coupled[0] - LOSS_FACTOR * coupled[1])
    imag_out = diag_real * values[1] + diag_imag * values[0] - (coupled[1] + LOSS_FACTOR * coupled[0])
    return jnp.stack([real_out, imag_out])


def right_product(left_real, left_imag, right_real, right_imag):
    def matmul(first, second):
        return jnp.einsum('hij,hkj->hik', first, second, precision=lax.Precision.HIGHEST)
    return (matmul(left_real, right_real) - matmul(left_imag, right_imag),
            matmul(left_real, right_imag) + matmul(left_imag, right_real))


def left_product(left_real, left_imag, right_real, right_imag):
    def matmul(first, second):
        return jnp.einsum('hij,hjk->hik', first, second, precision=lax.Precision.HIGHEST)
    return (matmul(left_real, right_real) - matmul(left_imag, right_imag),
            matmul(left_real, right_imag) + matmul(left_imag, right_real))


def jacobi_step(residual, diag_real, diag_imag):
    scale = RELAXATION / (diag_real * diag_real + diag_imag * diag_imag)
    real_out = (diag_real * residual[0] + diag_imag * residual[1]) * scale
    imag_out = (diag_real * residual[1] - diag_imag * residual[0]) * scale
    return jnp.stack([real_out, imag_out])


def restrict(residual, rows, cols):
    shape = residual.shape
    blocks = residual.reshape(2, shape[1], shape[2], rows, AR, cols, AA)
    return jnp.sum(blocks, axis=(2, 4, 6))


def prolong(coarse_values):
    spread = jnp.repeat(jnp.repeat(coarse_values, AR, axis=2), AA, axis=3)
    return spread[:, :, None]


def pad_field(values):
    return jnp.pad(values, ((0, 0), (0, 0), (0, 0), (1, 1), (1, 1)))


def reference(rhs, mat_ids, stiff_table, dens_table, mass_shift, harmonic, radial_factor, axial_factor):
    stiffness = material(mat_ids, stiff_table)
    density = material(mat_ids, dens_table)
    padded_stiff = jnp.pad(stiffness, ((0, 0), (1, 1), (1, 1)))
    weights = couplings(stiffness, padded_stiff)
    total = weights[0] + weights[1] + weights[2] + weights[3] + weights[4] + weights[5]
    diag_real = total[None] - mass_shift[:, None, None, None] * density[None]
    diag_imag = LOSS_FACTOR * total
    angles = (2.0 * jnp.pi / NSECT) * harmonic.astype(rhs.dtype)
    cosines = jnp.cos(angles)
    sines = jnp.sin(angles)
    solution = jnp.zeros_like(rhs)
    residual = rhs
    for iteration in range(ITERS):
        if iteration > 0:
            residual = rhs - operate(solution, pad_field(solution), weights, diag_real, diag_imag, cosines, sines)
        coarse_res = restrict(residual, GR, GA)
        mixed_real, mixed_imag = right_product(coarse_res[0], coarse_res[1], axial_factor[0], axial_factor[1])
        corr_real, corr_imag = left_product(radial_factor[0], radial_factor[1], mixed_real, mixed_imag)
        solution = solution + jacobi_step(residual, diag_real, diag_imag) + prolong(jnp.stack([corr_real, corr_imag]))
    residual = rhs - operate(solution, pad_field(solution), weights, diag_real, diag_imag, cosines, sines)
    return solution, residual
```

```python
import functools

import jax
import jax.numpy as jnp
from jax import lax
from jax.experimental import pallas as pl
from jax.experimental.pallas import tpu as pltpu
from jax.sharding import PartitionSpec as P

ITERS = 3
NSECT = 24
AR = 4
AA = 8
LOSS_FACTOR = 0.2
RELAXATION = 0.6
MESH = pl.DeviceIdType.MESH
HIGHEST = lax.Precision.HIGHEST
CHUNK = 8


def kernel(
    nrad,
    nax,
    rhs_hbm,
    ids_hbm,
    stiff_hbm,
    dens_hbm,
    mass_hbm,
    harm_hbm,
    radial_hbm,
    axial_hbm,
    sol_ref,
    res_ref,
    rhs_ref,
    ids_ref,
    stiff_ref,
    dens_ref,
    mass_ref,
    harm_ref,
    radial_ref,
    axial_ref,
    in_sem,
    stiff,
    wr_up,
    wr_dn,
    wa_lo,
    wa_hi,
    wt,
    dr,
    di,
    sc,
    srow_s,
    srow_r,
    scol_s,
    scol_r,
    row_s,
    row_r,
    col_s,
    col_r,
    col_m,
    one_s,
    one_r,
    two_r,
    axmat,
    radmat,
    st_send,
    st_recv,
    ha_send,
    ha_recv,
    g1_send,
    g1_recv,
    g2_send,
    g2_recv,
):
    loads = [
        pltpu.make_async_copy(src, dst, in_sem.at[n])
        for n, (src, dst) in enumerate(
            (
                (stiff_hbm, stiff_ref),
                (ids_hbm, ids_ref),
                (rhs_hbm, rhs_ref),
                (dens_hbm, dens_ref),
                (mass_hbm, mass_ref),
                (harm_hbm, harm_ref),
                (radial_hbm, radial_ref),
                (axial_hbm, axial_ref),
            )
        )
    ]
    for load_in in loads:
        load_in.start()
    ct = rhs_ref.shape[2]
    rows, lanes = rhs_ref.shape[3:]
    gr = radial_ref.shape[2]
    ga = axial_ref.shape[2]
    band_r = rows // AR
    band_c = lanes // AA
    i = lax.axis_index("radial")
    j = lax.axis_index("axial")
    has_up, has_dn = i > 0, i < nrad - 1
    has_lo, has_hi = j > 0, j < nax - 1
    conds = (has_up, has_dn, has_lo, has_hi)
    targets = ({"radial": i - 1}, {"radial": i + 1}, {"axial": j - 1}, {"axial": j + 1})

    for d in range(4):

        @pl.when(jnp.logical_not(conds[d]))
        def _():
            if d < 2:
                srow_r[d] = jnp.zeros(srow_r.shape[1:], jnp.float32)
                for k in range(ITERS):
                    row_r[k, d] = jnp.zeros(row_r.shape[2:], jnp.float32)
            else:
                scol_r[d - 2] = jnp.zeros(scol_r.shape[1:], jnp.float32)
                for k in range(ITERS):
                    col_r[k, d - 2] = jnp.zeros(col_r.shape[2:], jnp.float32)

    barrier = pltpu.get_barrier_semaphore()
    for d in range(1, nax):
        pl.semaphore_signal(
            barrier, inc=1, device_id={"axial": lax.rem(j + d, nax)}, device_id_type=MESH
        )
    for d in range(1, nrad):
        pl.semaphore_signal(
            barrier, inc=1, device_id={"radial": lax.rem(i + d, nrad)}, device_id_type=MESH
        )

    row = lax.broadcasted_iota(jnp.int32, (rows, lanes), 0)
    lane = lax.broadcasted_iota(jnp.int32, (rows, lanes), 1)
    zero = jnp.zeros((rows, lanes), jnp.float32)

    def lookup(ids, table):
        value = jnp.full(ids.shape, table[0], jnp.float32)
        for entry in range(1, table.shape[0]):
            value = jnp.where(ids == entry, table[entry], value)
        return value

    cap = lanes // 2
    pair = lane // 2

    def pack(value, t, packed):
        at = lax.rem(t, cap)
        return jnp.where(pair == at, pltpu.roll(value, 2 * at + 1, 1), packed)

    def stiff_copy(d):
        if d < 2:
            src, dst = srow_s.at[d], srow_r.at[1 - d]
        else:
            src, dst = scol_s, scol_r.at[3 - d]
        return pltpu.make_async_remote_copy(
            src_ref=src,
            dst_ref=dst,
            send_sem=st_send.at[d],
            recv_sem=st_recv.at[d ^ 1],
            device_id=targets[d],
            device_id_type=MESH,
        )

    middle = 3 * (ct // CHUNK) // 4

    def halo_copy(k, d, late=1):
        if d < 2:
            part = pl.ds(middle * CHUNK, ct - middle * CHUNK) if late else pl.ds(0, middle * CHUNK)
            src, dst = row_s.at[k, d, :, part], row_r.at[k, 1 - d, :, part]
        else:
            src, dst = col_s.at[k], col_r.at[k, 3 - d]
        return pltpu.make_async_remote_copy(
            src_ref=src,
            dst_ref=dst,
            send_sem=ha_send.at[k, late, d],
            recv_sem=ha_recv.at[k, late, d ^ 1],
            device_id=targets[d],
            device_id_type=MESH,
        )

    def gather_one(k, d):
        return pltpu.make_async_remote_copy(
            src_ref=one_s.at[k],
            dst_ref=one_r.at[k, j],
            send_sem=g1_send.at[k, d],
            recv_sem=g1_recv.at[k, d],
            device_id={"axial": lax.rem(j + d, nax)},
            device_id_type=MESH,
        )

    def gather_two(k, d):
        return pltpu.make_async_remote_copy(
            src_ref=two_r.at[k, i],
            dst_ref=two_r.at[k, i],
            send_sem=g2_send.at[k, d],
            recv_sem=g2_recv.at[k, d],
            device_id={"radial": lax.rem(i + d, nrad)},
            device_id_type=MESH,
        )

    def on_faces(act, faces=4):
        for d in range(faces):

            @pl.when(conds[d])
            def _():
                act(d)

    scol_s[...] = jnp.zeros(scol_s.shape, jnp.float32)
    col_s[...] = jnp.zeros(col_s.shape, jnp.float32)
    loads[0].wait()
    loads[1].wait()

    @pl.loop(0, ct // CHUNK)
    def _(chunk):
        begin = chunk * CHUNK
        tile = begin // cap
        packed = scol_s[tile]
        for u in range(CHUNK):
            t = begin + u
            value = lookup(ids_ref[t], stiff_ref)
            stiff[t + 1] = value
            srow_s[0, pl.ds(t, 1), :] = value[0:1]
            srow_s[1, pl.ds(t, 1), :] = value[rows - 1 : rows]
            packed = pack(value, t, packed)
        scol_s[tile] = packed

    stiff[0] = stiff[ct]
    stiff[ct + 1] = stiff[1]

    pl.semaphore_wait(barrier, nax + nrad - 2)
    on_faces(lambda d: stiff_copy(d).start())

    e_row = lax.broadcasted_iota(jnp.int32, (lanes, lanes), 0)
    e_col = lax.broadcasted_iota(jnp.int32, (lanes, lanes), 1)
    fold = jnp.where(e_row // AA + j * band_c == e_col, 1.0, 0.0)

    def restrict_and_send(k, sums):
        tile = zero
        for c in range(4):
            s = sums[c] + pltpu.roll(sums[c], rows - 1, 0)
            s = s + pltpu.roll(s, rows - 2, 0)
            for g in range(band_r):
                to = c * band_r + g
                moved = pltpu.roll(s, (to - g * AR) % rows, 0)
                tile = jnp.where(row == to, moved, tile)
        one_s[k] = jnp.dot(tile, fold, precision=HIGHEST, preferred_element_type=jnp.float32)
        for d in range(1, nax):
            gather_one(k, d).start()

    loads[2].wait()

    def sum_pass(chunk, sums):
        sums = list(sums)
        for u in range(CHUNK):
            for c in range(4):
                sums[c] = sums[c] + rhs_ref[c // 2, c % 2, chunk * CHUNK + u]
        return tuple(sums)

    restrict_and_send(0, lax.fori_loop(0, ct // CHUNK, sum_pass, (zero,) * 4))
    for load_in in loads[3:]:
        load_in.wait()

    ax_row = lax.broadcasted_iota(jnp.int32, (lanes, ga), 0)
    ax_col = lax.broadcasted_iota(jnp.int32, (lanes, ga), 1)
    own = jnp.where(ax_row // AA + j * band_c == ax_col, 1.0, 0.0)
    edge_lo = j * band_c - 1
    edge_hi = (j + 1) * band_c
    half = lanes // 2
    edges = []
    for p in range(2):
        hit = ((ax_row == p * half) & (ax_col == edge_lo)) | (
            (ax_row == p * half + 1) & (ax_col == edge_hi)
        )
        edges.append(jnp.where(hit, 1.0, 0.0))
    for h in range(2):
        if ga < lanes:
            axmat[h] = jnp.zeros(axmat.shape[1:], jnp.float32)

        def spread(select, p):
            return jnp.dot(
                select, axial_ref[p, h], precision=HIGHEST, preferred_element_type=jnp.float32
            )

        axmat[h, 0:lanes, 0:ga] = spread(own, 0)
        axmat[h, lanes : 2 * lanes, 0:ga] = spread(own, 1)
        axmat[h, 2 * lanes : 3 * lanes, 0:ga] = spread(edges[0], 0) + spread(edges[1], 1)

    per = 2 * rows
    cdev = 4 * band_r
    r_row = lax.broadcasted_iota(jnp.int32, (4 * per, gr), 0) % per
    r_col = lax.broadcasted_iota(jnp.int32, (4 * per, gr), 1)
    want = jnp.where(
        r_row < rows,
        r_row // AR + i * band_r,
        jnp.where(
            r_row == rows, i * band_r - 1, jnp.where(r_row == rows + 1, (i + 1) * band_r, -1)
        ),
    )
    r_sel = jnp.where(want == r_col, 1.0, 0.0)
    c_row = lax.broadcasted_iota(jnp.int32, (gr, nrad * cdev), 0)
    c_col = lax.broadcasted_iota(jnp.int32, (gr, nrad * cdev), 1)
    c_sel = jnp.where((c_col // cdev) * band_r + c_col % band_r == c_row, 1.0, 0.0)
    m_out = lax.broadcasted_iota(jnp.int32, (4 * per, nrad * cdev), 0) // per
    m_in = (lax.broadcasted_iota(jnp.int32, (4 * per, nrad * cdev), 1) % cdev) // band_r
    built = jnp.zeros((4 * per, nrad * cdev), jnp.float32)
    for h in range(2):
        for p in range(2):
            part = jnp.dot(
                jnp.dot(
                    r_sel, radial_ref[p, h], precision=HIGHEST, preferred_element_type=jnp.float32
                ),
                c_sel,
                precision=HIGHEST,
                preferred_element_type=jnp.float32,
            )
            if p == 0:
                built = jnp.where((m_out == m_in) & (m_out % 2 == h), part, built)
            else:
                built = jnp.where((m_out == h) & (m_in == 2 + h), -part, built)
                built = jnp.where((m_out == 2 + h) & (m_in == h), part, built)
    radmat[...] = built

    def mix_and_send(k):
        total = one_s[k]
        for d in range(1, nax):
            gather_one(k, d).wait_recv()
        for d in range(1, nax):
            total = total + one_r[k, lax.rem(j + d, nax)]
        outs = []
        for h in range(2):
            prod = lax.dot_general(
                total,
                axmat[h],
                (((1,), (1,)), ((), ())),
                precision=HIGHEST,
                preferred_element_type=jnp.float32,
            )
            a = prod[:, 0:lanes]
            b = prod[:, lanes : 2 * lanes]
            e = prod[:, 2 * lanes : 3 * lanes]
            f = pltpu.roll(e, half, 1)
            swap_b = pltpu.roll(b, rows // 2, 0)
            swap_f = pltpu.roll(f, rows // 2, 0)
            low = row < rows // 2
            outs.append(
                (jnp.where(low, a - swap_b, a + swap_b), jnp.where(low, e - swap_f, e + swap_f))
            )
        odd = (row // band_r) % 2 == 1
        two_r[k, i, :, 0:lanes] = jnp.where(odd, outs[1][0], outs[0][0])
        two_r[k, i, :, lanes : 2 * lanes] = jnp.where(odd, outs[1][1], outs[0][1])
        for d in range(1, nrad):
            gather_two(k, d).start()

    def finish_coarse(k):
        for d in range(1, nrad):
            gather_two(k, d).wait_recv()
        return jnp.dot(
            radmat[...],
            two_r[k].reshape(nrad * cdev, 2 * lanes),
            precision=HIGHEST,
            preferred_element_type=jnp.float32,
        )

    mix_and_send(0)
    on_faces(lambda d: stiff_copy(d ^ 1).wait_recv())

    mass = [mass_ref[0], mass_ref[1]]

    odd_lane = lane % 2 == 1

    def around(value, up, dn, beside, t):
        edge = pltpu.roll(beside, lanes - 1 - 2 * lax.rem(t, cap), 1)
        return (
            jnp.where(row == 0, up, pltpu.roll(value, 1, 0)),
            jnp.where(row == rows - 1, dn, pltpu.roll(value, rows - 1, 0)),
            pltpu.roll(jnp.where(lane == lanes - 1, edge, value), 1, 1),
            pltpu.roll(jnp.where(lane == 0, edge, value), lanes - 1, 1),
        )

    def put_rows(k, t, y):
        for c in range(4):
            row_s[k, 0, c, pl.ds(t, 1), :] = y[c][0:1]
            row_s[k, 1, c, pl.ds(t, 1), :] = y[c][rows - 1 : rows]

    def smooth(t, rr, ri, h):
        d_re, d_im, scale = dr[h, t], di[t], sc[h, t]
        return (d_re * rr + d_im * ri) * scale, (d_re * ri - d_im * rr) * scale

    for n in range(scol_s.shape[0]):
        col_m[0, n] = jnp.where(odd_lane, scol_r[1, n], scol_r[0, n])

    def setup_step(t, packs, beside):
        value = stiff[t + 1]
        up, dn, lo, hi = around(
            value,
            srow_r[0, pl.ds(t, 1), :],
            srow_r[1, pl.ds(t, 1), :],
            beside,
            t,
        )
        c_up, c_dn = 0.5 * (value + up), 0.5 * (value + dn)
        c_lo, c_hi = 0.5 * (value + lo), 0.5 * (value + hi)
        c_be, c_ah = 0.5 * (value + stiff[t]), 0.5 * (value + stiff[t + 2])
        wr_up[t] = c_up
        wr_dn[t] = c_dn
        wa_lo[t] = c_lo
        wa_hi[t] = c_hi
        wt[t] = c_be
        wt[t + 1] = c_ah
        total = c_dn + c_up + c_hi + c_lo + c_ah + c_be
        density = lookup(ids_ref[t], dens_ref)
        d_im = LOSS_FACTOR * total
        di[t] = d_im
        y = [None] * 4
        for h in range(2):
            d_re = total - mass[h] * density
            scale = RELAXATION / (d_re * d_re + d_im * d_im)
            dr[h, t] = d_re
            sc[h, t] = scale
            rr, ri = rhs_ref[0, h, t], rhs_ref[1, h, t]
            y[h] = (d_re * rr + d_im * ri) * scale
            y[2 + h] = (d_re * ri - d_im * rr) * scale
            sol_ref[0, h, t] = y[h]
            sol_ref[1, h, t] = y[2 + h]
        put_rows(0, t, y)
        return [pack(y[c], t, packs[c]) for c in range(4)]

    def setup_chunk(chunk, nothing):
        begin = chunk * CHUNK
        tile = begin // cap
        beside = col_m[0, tile]
        packs = [col_s[0, c, tile] for c in range(4)]
        for u in range(CHUNK):
            packs = setup_step(begin + u, packs, beside)
        for c in range(4):
            col_s[0, c, tile] = packs[c]
        return nothing

    lax.fori_loop(0, middle, setup_chunk, 0)
    on_faces(lambda d: halo_copy(0, d, 0).start(), 2)
    lax.fori_loop(middle, ct // CHUNK, setup_chunk, 0)
    on_faces(lambda d: halo_copy(0, d).start())

    cosines, sines = [], []
    for h in range(2):
        angle = jnp.full((rows, lanes), harm_ref[h], jnp.int32).astype(jnp.float32) * (
            2.0 * jnp.pi / NSECT
        )
        cosines.append(jnp.cos(angle))
        sines.append(jnp.sin(angle))

    for k in range(ITERS):
        final = k == ITERS - 1
        coarse = finish_coarse(k)
        corr = [coarse[c * per : c * per + rows, 0:lanes] for c in range(4)]
        on_faces(lambda d: halo_copy(k, d ^ 1, 0).wait_recv(), 2)
        on_faces(lambda d: halo_copy(k, d ^ 1).wait_recv())
        for c in range(4):
            add = []
            for side in range(2):
                at = c * per + rows + side
                row_r[k, side, c] = row_r[k, side, c] + coarse[at : at + 1, 0:lanes]
                add.append(coarse[c * per : c * per + rows, lanes + side : lanes + side + 1])
            for n in range(col_m.shape[1]):
                col_m[c, n] = jnp.where(
                    odd_lane, col_r[k, 1, c, n] + add[1], col_r[k, 0, c, n] + add[0]
                )

        def load(t):
            return [sol_ref[c // 2, c % 2, t] + corr[c] for c in range(4)]

        def turn(x, sign):
            return [cosines[h] * x[h] - sign * sines[h] * x[2 + h] for h in range(2)] + [
                sign * sines[h] * x[h] + cosines[h] * x[2 + h] for h in range(2)
            ]

        start = load(0)
        beyond = turn(start, 1.0)
        before = turn(load(ct - 1), -1.0)

        def stencil(t, xm, x, xp, beside):
            c_up, c_dn, c_lo, c_hi = wr_up[t], wr_dn[t], wa_lo[t], wa_hi[t]
            c_be, c_ah = wt[t], wt[t + 1]
            nb = []
            for c in range(4):
                up, dn, lo, hi = around(
                    x[c],
                    row_r[k, 0, c, pl.ds(t, 1), :],
                    row_r[k, 1, c, pl.ds(t, 1), :],
                    beside[c],
                    t,
                )
                nb.append(
                    (c_dn * dn + c_up * up)
                    + (c_hi * hi + c_lo * lo)
                    + (c_ah * xp[c] + c_be * xm[c])
                )
            d_im = di[t]
            res = [None] * 4
            for h in range(2):
                d_re = dr[h, t]
                re, im = h, 2 + h
                res[re] = rhs_ref[0, h, t] - (
                    d_re * x[re] - d_im * x[im] - (nb[re] - LOSS_FACTOR * nb[im])
                )
                res[im] = rhs_ref[1, h, t] - (
                    d_re * x[im] + d_im * x[re] - (nb[im] + LOSS_FACTOR * nb[re])
                )
            return res

        def chunk_pass(chunk, carry):
            xm, x, sums = list(carry[0:4]), list(carry[4:8]), list(carry[8:])
            begin = chunk * CHUNK
            tile = begin // cap
            beside = [col_m[c, tile] for c in range(4)]
            if not final:
                packs = [col_s[k + 1, c, tile] for c in range(4)]
            for u in range(CHUNK):
                t = begin + u
                if u < CHUNK - 1:
                    xp = load(t + 1)
                else:
                    ended = t == ct - 1
                    xp = load(jnp.minimum(t + 1, ct - 1))
                    xp = [jnp.where(ended, beyond[c], xp[c]) for c in range(4)]
                res = stencil(t, xm, x, xp, beside)
                if final:
                    for c in range(4):
                        sol_ref[c // 2, c % 2, t] = x[c]
                        res_ref[c // 2, c % 2, t] = res[c]
                else:
                    y = [None] * 4
                    for h in range(2):
                        a, b = smooth(t, res[h], res[2 + h], h)
                        y[h], y[2 + h] = x[h] + a, x[2 + h] + b
                    for c in range(4):
                        sol_ref[c // 2, c % 2, t] = y[c]
                        sums[c] = sums[c] + res[c]
                        packs[c] = pack(y[c], t, packs[c])
                    put_rows(k + 1, t, y)
                xm, x = x, xp
            if not final:
                for c in range(4):
                    col_s[k + 1, c, tile] = packs[c]
            return tuple(xm) + tuple(x) + tuple(sums)

        state = () if final else (zero,) * 4
        carry = tuple(before) + tuple(start) + state
        if final:
            lax.fori_loop(0, ct // CHUNK, chunk_pass, carry)
        else:
            carry = lax.fori_loop(0, middle, chunk_pass, carry)
            on_faces(lambda d: halo_copy(k + 1, d, 0).start(), 2)
            carry = lax.fori_loop(middle, ct // CHUNK, chunk_pass, carry)
        if not final:
            restrict_and_send(k + 1, carry[8:])
            on_faces(lambda d: halo_copy(k + 1, d).start())
            mix_and_send(k + 1)

    on_faces(lambda d: stiff_copy(d).wait_send())
    for k in range(ITERS):
        on_faces(lambda d: halo_copy(k, d, 0).wait_send(), 2)
        on_faces(lambda d: halo_copy(k, d).wait_send())
        for d in range(1, nax):
            gather_one(k, d).wait_send()
        for d in range(1, nrad):
            gather_two(k, d).wait_send()


def local(rhs, mat_ids, stiff_table, dens_table, mass_shift, harmonic, radial_factor, axial_factor):
    nrad = lax.axis_size("radial")
    nax = lax.axis_size("axial")
    ct, rows, lanes = mat_ids.shape
    vmem = pl.BlockSpec(memory_space=pltpu.VMEM)
    hbm = pl.BlockSpec(memory_space=pltpu.HBM)
    tiles = -(-2 * ct // lanes)
    f32 = jnp.float32
    field = (ct, rows, lanes)
    cdev = 4 * (rows // AR)
    dma = pltpu.SemaphoreType.DMA
    sol, res = pl.pallas_call(
        functools.partial(kernel, nrad, nax),
        out_shape=(pltpu.VMEM(rhs.shape, f32), pltpu.VMEM(rhs.shape, f32)),
        in_specs=[hbm] * 8,
        out_specs=(vmem, vmem),
        scratch_shapes=[
            pltpu.VMEM(rhs.shape, f32),
            pltpu.VMEM(field, jnp.int32),
            pltpu.SMEM(stiff_table.shape, f32),
            pltpu.SMEM(dens_table.shape, f32),
            pltpu.SMEM(mass_shift.shape, f32),
            pltpu.SMEM(harmonic.shape, jnp.int32),
            pltpu.VMEM(radial_factor.shape, f32),
            pltpu.VMEM(axial_factor.shape, f32),
            dma((8,)),
            pltpu.VMEM((ct + 2, rows, lanes), f32),
            pltpu.VMEM(field, f32),
            pltpu.VMEM(field, f32),
            pltpu.VMEM(field, f32),
            pltpu.VMEM(field, f32),
            pltpu.VMEM((ct + 1, rows, lanes), f32),
            pltpu.VMEM((2,) + field, f32),
            pltpu.VMEM(field, f32),
            pltpu.VMEM((2,) + field, f32),
            pltpu.VMEM((2, ct, lanes), f32),
            pltpu.VMEM((2, ct, lanes), f32),
            pltpu.VMEM((tiles, rows, lanes), f32),
            pltpu.VMEM((2, tiles, rows, lanes), f32),
            pltpu.VMEM((ITERS, 2, 4, ct, lanes), f32),
            pltpu.VMEM((ITERS, 2, 4, ct, lanes), f32),
            pltpu.VMEM((ITERS, 4, tiles, rows, lanes), f32),
            pltpu.VMEM((ITERS, 2, 4, tiles, rows, lanes), f32),
            pltpu.VMEM((4, tiles, rows, lanes), f32),
            pltpu.VMEM((ITERS, rows, lanes), f32),
            pltpu.VMEM((ITERS, nax, rows, lanes), f32),
            pltpu.VMEM((ITERS, nrad, rows, 2 * lanes), f32),
            pltpu.VMEM((2, 3 * lanes, lanes), f32),
            pltpu.VMEM((8 * rows, nrad * cdev), f32),
            dma((4,)),
            dma((4,)),
            dma((ITERS, 2, 4)),
            dma((ITERS, 2, 4)),
            dma((ITERS, nax)),
            dma((ITERS, nax)),
            dma((ITERS, nrad)),
            dma((ITERS, nrad)),
        ],
        compiler_params=pltpu.CompilerParams(
            collective_id=0, has_side_effects=True, vmem_limit_bytes=40 * 1024 * 1024
        ),
    )(*[pltpu.with_memory_space_constraint(x, pltpu.HBM) for x in (rhs, mat_ids, stiff_table, dens_table, mass_shift, harmonic, radial_factor, axial_factor)])
    return pl.pallas_call(
        put_out,
        out_shape=(jax.ShapeDtypeStruct(rhs.shape, f32), jax.ShapeDtypeStruct(rhs.shape, f32)),
        in_specs=[vmem] * 2,
        out_specs=(hbm, hbm),
        scratch_shapes=[dma((2, 4))],
    )(pltpu.with_memory_space_constraint(sol, pltpu.VMEM), pltpu.with_memory_space_constraint(res, pltpu.VMEM))


def put_out(a_ref, b_ref, x_ref, y_ref, sem):
    copies = []
    for n, (src, dst) in enumerate(((a_ref, x_ref), (b_ref, y_ref))):
        for c in range(4):
            copies.append(pltpu.make_async_copy(src.at[c // 2, c % 2], dst.at[c // 2, c % 2], sem.at[n, c]))
    for c in copies:
        c.start()
    for c in copies:
        c.wait()


def solution(mesh):
    return jax.shard_map(
        local,
        mesh=mesh,
        in_specs=(
            P(None, None, None, "radial", "axial"),
            P(None, "radial", "axial"),
            P(),
            P(),
            P(),
            P(),
            P(),
            P(),
        ),
        out_specs=(P(None, None, None, "radial", "axial"), P(None, None, None, "radial", "axial")),
        check_vma=False,
    )
```

```python
import functools

import jax
import jax.numpy as jnp
from jax import lax
from jax.experimental import pallas as pl
from jax.experimental.pallas import tpu as pltpu
from jax.sharding import PartitionSpec as P

ITERS = 3
NSECT = 24
AR = 4
AA = 8
LOSS_FACTOR = 0.2
RELAXATION = 0.6
MESH = pl.DeviceIdType.MESH
HIGHEST = lax.Precision.HIGHEST
CHUNK = 8
PARTS = 4
GROUP = 32


def dot(a, b):
    return jnp.dot(a, b, precision=HIGHEST, preferred_element_type=jnp.float32)


def grid_of(rows, lanes):
    return (
        lax.broadcasted_iota(jnp.int32, (rows, lanes), 0),
        lax.broadcasted_iota(jnp.int32, (rows, lanes), 1),
    )


def around(value, up, dn, edge):
    rows, lanes = value.shape
    row, lane = grid_of(rows, lanes)
    return (
        jnp.where(row == 0, up, pltpu.roll(value, 1, 0)),
        jnp.where(row == rows - 1, dn, pltpu.roll(value, rows - 1, 0)),
        pltpu.roll(jnp.where(lane == lanes - 1, edge, value), 1, 1),
        pltpu.roll(jnp.where(lane == 0, edge, value), lanes - 1, 1),
    )


def lossy(x):
    return [x[h] - LOSS_FACTOR * x[2 + h] for h in range(2)] + [
        x[2 + h] + LOSS_FACTOR * x[h] for h in range(2)
    ]


def coarse_change(weights, push, c):
    w_up, w_dn, w_lo, w_hi, dens = weights
    return ((w_up * push[0][c] + w_dn * push[1][c]) + (w_lo * push[2][c] + w_hi * push[3][c])) - (
        dens * push[4][c]
    )


def turn(trig, x, sign):
    cosines, sines = trig[0:2], trig[2:4]
    return [cosines[h] * x[h] - sign * sines[h] * x[2 + h] for h in range(2)] + [
        sign * sines[h] * x[h] + cosines[h] * x[2 + h] for h in range(2)
    ]


def kernel(
    nrad,
    nax,
    rhs_hbm,
    ids_hbm,
    stiff_hbm,
    dens_hbm,
    mass_hbm,
    harm_hbm,
    radial_hbm,
    axial_hbm,
    sol_ref,
    val_ref,
    wr_up,
    wr_dn,
    wa_lo,
    wa_hi,
    dens,
    corr_ref,
    push_ref,
    rhs_ref,
    ids_ref,
    stiff_ref,
    dens_ref,
    mass_ref,
    harm_ref,
    radial_ref,
    axial_ref,
    in_sem,
    stiff,
    wt,
    dr,
    di,
    sc,
    edge_ref,
    srow_s,
    srow_r,
    scol_s,
    scol_r,
    scol_m,
    row_r,
    col_s,
    col_r,
    all_r,
    axmat,
    radmat,
    st_send,
    st_recv,
    ha_send,
    ha_recv,
    ga_send,
    ga_recv,
):
    loads = [
        pltpu.make_async_copy(src, dst, in_sem.at[n])
        for n, (src, dst) in enumerate(
            (
                (stiff_hbm, stiff_ref),
                (ids_hbm, ids_ref),
                (rhs_hbm, rhs_ref),
                (dens_hbm, dens_ref),
                (mass_hbm, mass_ref),
                (harm_hbm, harm_ref),
                (radial_hbm, radial_ref),
                (axial_hbm, axial_ref),
            )
        )
    ]
    for load_in in loads:
        load_in.start()
    ct = rhs_ref.shape[2]
    rows, lanes = rhs_ref.shape[3:]
    gr = radial_ref.shape[2]
    ga = axial_ref.shape[2]
    band_r = rows // AR
    band_c = lanes // AA
    chunks = ct // CHUNK
    ndev = nrad * nax
    i = lax.axis_index("radial")
    j = lax.axis_index("axial")
    me = i * nax + j
    has_up, has_dn = i > 0, i < nrad - 1
    has_lo, has_hi = j > 0, j < nax - 1
    conds = (has_up, has_dn, has_lo, has_hi)
    targets = ({"radial": i - 1}, {"radial": i + 1}, {"axial": j - 1}, {"axial": j + 1})

    def peer(d):
        at = lax.rem(me + d, ndev)
        return {"radial": at // nax, "axial": lax.rem(at, nax)}

    barrier = pltpu.get_barrier_semaphore()

    @pl.loop(1, ndev)
    def _(d):
        pl.semaphore_signal(barrier, inc=1, device_id=peer(d), device_id_type=MESH)

    for d in range(4):

        @pl.when(jnp.logical_not(conds[d]))
        def _():
            if d < 2:
                srow_r[d] = jnp.zeros(srow_r.shape[1:], jnp.float32)
                for k in range(ITERS):
                    row_r[k, d] = jnp.zeros(row_r.shape[2:], jnp.float32)
            else:
                scol_r[d - 2] = jnp.zeros(scol_r.shape[1:], jnp.float32)
                for k in range(ITERS):
                    col_r[k, d - 2] = jnp.zeros(col_r.shape[2:], jnp.float32)

    row, lane = grid_of(rows, lanes)
    zero = jnp.zeros((rows, lanes), jnp.float32)
    pair = lane // 2
    odd_lane = lane % 2 == 1

    def lookup(ids, table):
        value = jnp.full(ids.shape, table[0], jnp.float32)
        for entry in range(1, table.shape[0]):
            value = jnp.where(ids == entry, table[entry], value)
        return value

    def pack(value, at, packed):
        return jnp.where(pair == at, pltpu.roll(value, (2 * at + 1) % lanes, 1), packed)

    def stiff_copy(d):
        if d < 2:
            src, dst = srow_s.at[d], srow_r.at[1 - d]
        else:
            src, dst = scol_s, scol_r.at[3 - d]
        return pltpu.make_async_remote_copy(
            src_ref=src,
            dst_ref=dst,
            send_sem=st_send.at[d],
            recv_sem=st_recv.at[d ^ 1],
            device_id=targets[d],
            device_id_type=MESH,
        )

    part_chunks = chunks // PARTS
    part_ct = ct // PARTS

    def halo_copy(k, part, d):
        if d < 2:
            at = pl.ds(part * part_ct, part_ct)
            line = pl.ds(0 if d == 0 else rows - 1, 1)
            src, dst = sol_ref.at[:, :, at, line], row_r.at[k, 1 - d, :, :, at]
        else:
            at = pl.ds(part * part_chunks, part_chunks)
            src, dst = col_s.at[k, at], col_r.at[k, 3 - d, at]
        return pltpu.make_async_remote_copy(
            src_ref=src,
            dst_ref=dst,
            send_sem=ha_send.at[k, part, d],
            recv_sem=ha_recv.at[k, part, d ^ 1],
            device_id=targets[d],
            device_id_type=MESH,
        )

    def gather(k, d):
        return pltpu.make_async_remote_copy(
            src_ref=all_r.at[k, me],
            dst_ref=all_r.at[k, me],
            send_sem=ga_send.at[k, d],
            recv_sem=ga_recv.at[k, d],
            device_id=peer(d),
            device_id_type=MESH,
        )

    def on_faces(act):
        for d in range(4):

            @pl.when(conds[d])
            def _():
                act(d)

    loads[0].wait()
    loads[1].wait()

    @pl.loop(0, ct // GROUP)
    def _(group):
        packed = zero
        for u in range(GROUP):
            t = group * GROUP + u
            value = lookup(ids_ref[t], stiff_ref)
            stiff[t + 1] = value
            srow_s[0, pl.ds(t, 1), :] = value[0:1]
            srow_s[1, pl.ds(t, 1), :] = value[rows - 1 : rows]
            packed = pack(value, u, packed)
        scol_s[group] = packed

    stiff[0] = stiff[ct]
    stiff[ct + 1] = stiff[1]

    pl.semaphore_wait(barrier, ndev - 1)
    on_faces(lambda d: stiff_copy(d).start())

    e_row, e_col = grid_of(lanes, lanes)
    fold = jnp.where(e_row // AA == e_col % band_c, 1.0, 0.0)
    k_row, k_col = grid_of(4 * rows, lanes)
    keep = k_row // AR == (j + rows - k_col // band_c) % rows

    def restrict_and_send(k, sums):
        folded = dot(jnp.concatenate(sums, axis=0), fold)
        all_r[k, me] = jnp.sum(jnp.where(keep, folded, 0.0), axis=0, keepdims=True)

        @pl.loop(1, ndev)
        def _(d):
            gather(k, d).start()

    loads[2].wait()

    def sum_pass(chunk, sums):
        sums = list(sums)
        for u in range(CHUNK):
            for c in range(4):
                sums[c] = sums[c] + rhs_ref[c // 2, c % 2, chunk * CHUNK + u]
        return tuple(sums)

    restrict_and_send(0, lax.fori_loop(0, chunks, sum_pass, (zero,) * 4))
    for load_in in loads[3:]:
        load_in.wait()

    ax_row, ax_col = grid_of(lanes, ga)
    own = jnp.where(ax_row // AA + j * band_c == ax_col, 1.0, 0.0)
    half = lanes // 2
    side = jnp.where(ax_row % 2 == 0, j * band_c - 1, (j + 1) * band_c) == ax_col
    edges = [jnp.where(side & (ax_row // half == p), 1.0, 0.0) for p in range(2)]
    for h in range(2):
        if ga < lanes:
            axmat[h] = jnp.zeros(axmat.shape[1:], jnp.float32)
        axmat[h, 0:lanes, 0:ga] = dot(own, axial_ref[0, h])
        axmat[h, lanes : 2 * lanes, 0:ga] = dot(own, axial_ref[1, h])
        axmat[h, 2 * lanes : 3 * lanes, 0:ga] = dot(edges[0], axial_ref[0, h]) + dot(
            edges[1], axial_ref[1, h]
        )

    per = 2 * rows
    cdev = 4 * band_r
    r_row, r_col = grid_of(4 * per, gr)
    r_row = r_row % per
    want = jnp.where(
        r_row < rows,
        r_row // AR + i * band_r,
        jnp.where(
            r_row == rows, i * band_r - 1, jnp.where(r_row == rows + 1, (i + 1) * band_r, -1)
        ),
    )
    r_sel = jnp.where(want == r_col, 1.0, 0.0)
    c_row, c_col = grid_of(gr, nrad * cdev)
    c_sel = jnp.where((c_col // cdev) * band_r + c_col % band_r == c_row, 1.0, 0.0)
    m_row, m_col = grid_of(4 * per, nrad * cdev)
    m_out = m_row // per
    m_in = (m_col % cdev) // band_r
    first = jnp.zeros((4 * per, nrad * cdev), jnp.float32)
    second = first
    for h in range(2):
        same = (m_out == m_in) & (m_out % 2 == h)
        to_re = (m_out == h) & (m_in == 2 + h)
        to_im = (m_out == 2 + h) & (m_in == h)
        real = dot(dot(r_sel, radial_ref[0, h]), c_sel)
        imag = dot(dot(r_sel, radial_ref[1, h]), c_sel)
        first = jnp.where(same, real, first)
        first = jnp.where(to_re, -imag, first)
        first = jnp.where(to_im, imag, first)
        second = jnp.where(same, -imag, second)
        second = jnp.where(to_re, -real, second)
        second = jnp.where(to_im, real, second)
    radmat[:, 0 : nrad * cdev] = first
    radmat[:, nrad * cdev : 2 * nrad * cdev] = second

    p_row, _ = grid_of(nrad * cdev, 3 * lanes)
    odd_harm = (p_row // band_r) % 2 == 1

    def finish_coarse(k):
        @pl.loop(1, ndev)
        def _(d):
            gather(k, d).wait_recv()

        tiles = []
        for a in range(nrad):
            tile = zero
            for b in range(nax):
                tile = jnp.where((lane // band_c + row) % rows == b, all_r[k, a * nax + b], tile)
            tile = pltpu.roll(tile, 0, 1, stride=band_c, stride_axis=0)
            tiles.append(tile)
        whole = jnp.concatenate(tiles, axis=0)
        prod = [
            lax.dot_general(
                whole,
                axmat[h],
                (((1,), (1,)), ((), ())),
                precision=HIGHEST,
                preferred_element_type=jnp.float32,
            )
            for h in range(2)
        ]
        prod = jnp.where(odd_harm, prod[1], prod[0])
        a = prod[:, 0:lanes]
        b = prod[:, lanes : 2 * lanes]
        e = prod[:, 2 * lanes : 3 * lanes]
        f = pltpu.roll(e, half, 1)
        mixed = jnp.concatenate(
            [jnp.concatenate([a, e], axis=1), jnp.concatenate([b, f], axis=1)], axis=0
        )
        return dot(radmat[...], mixed)

    on_faces(lambda d: stiff_copy(d ^ 1).wait_recv())

    mass = [mass_ref[0], mass_ref[1]]

    def smooth(t, rr, ri, h):
        d_re, d_im, scale = dr[h, t], di[t], sc[h, t]
        return (d_re * rr + d_im * ri) * scale, (d_re * ri - d_im * rr) * scale

    per_group = GROUP // CHUNK
    for n in range(ct // GROUP):
        merged = jnp.where(odd_lane, scol_r[1, n], scol_r[0, n])
        for m in range(per_group):
            scol_m[n * per_group + m] = (
                merged if m == 0 else pltpu.roll(merged, lanes - 2 * CHUNK * m, 1)
            )

    def setup_step(t, u, packed, beside, moved):
        value = stiff[t + 1]
        up, dn, lo, hi = around(
            value,
            srow_r[0, pl.ds(t, 1), :],
            srow_r[1, pl.ds(t, 1), :],
            pltpu.roll(beside, lanes - 1 - 2 * u, 1),
        )
        c_up, c_dn = 0.5 * (value + up), 0.5 * (value + dn)
        c_lo, c_hi = 0.5 * (value + lo), 0.5 * (value + hi)
        c_be, c_ah = 0.5 * (value + stiff[t]), 0.5 * (value + stiff[t + 2])
        wr_up[t] = c_up
        wr_dn[t] = c_dn
        wa_lo[t] = c_lo
        wa_hi[t] = c_hi
        wt[t] = c_be
        wt[t + 1] = c_ah
        total = c_dn + c_up + c_hi + c_lo + c_ah + c_be
        density = lookup(ids_ref[t], dens_ref)
        dens[t] = density
        moved = [m + w for m, w in zip(moved, (c_up, c_dn, c_lo, c_hi, density))]
        d_im = LOSS_FACTOR * total
        di[t] = d_im
        y = [None] * 4
        for h in range(2):
            d_re = total - mass[h] * density
            scale = RELAXATION / (d_re * d_re + d_im * d_im)
            dr[h, t] = d_re
            sc[h, t] = scale
            rr, ri = rhs_ref[0, h, t], rhs_ref[1, h, t]
            y[h] = (d_re * rr + d_im * ri) * scale
            y[2 + h] = (d_re * ri - d_im * rr) * scale
            sol_ref[0, h, t] = y[h]
            sol_ref[1, h, t] = y[2 + h]
        for c in range(4):
            packed = pack(y[c], c * CHUNK + u, packed)
        return packed, moved

    def in_parts(k, step, carry):
        def one_part(part, carry):
            carry = lax.fori_loop(
                0, part_chunks, lambda n, carry: step(part * part_chunks + n, carry), carry
            )
            on_faces(lambda d: halo_copy(k, part, d).start())
            return carry

        return lax.fori_loop(0, PARTS, one_part, carry)

    def setup_chunk(chunk, moved):
        packed = zero
        beside = scol_m[chunk]
        for u in range(CHUNK):
            packed, moved = setup_step(chunk * CHUNK + u, u, packed, beside, moved)
        col_s[0, chunk] = packed
        return tuple(moved)

    moved = in_parts(0, setup_chunk, (zero,) * 5)

    trig = [[], []]
    for h in range(2):
        angle = jnp.full((rows, lanes), harm_ref[h], jnp.int32).astype(jnp.float32) * (
            2.0 * jnp.pi / NSECT
        )
        trig[0].append(jnp.cos(angle))
        trig[1].append(jnp.sin(angle))
    trig = trig[0] + trig[1]

    def load(t):
        return [sol_ref[c // 2, c % 2, t] for c in range(4)]

    def apply_operator(k):
        start = load(0)
        beyond = turn(trig, start, 1.0)
        before = turn(trig, load(ct - 1), -1.0)

        def chunk_pass(chunk, carry):
            xm, x, sums = list(carry[0:4]), list(carry[4:8]), list(carry[8:])
            beside = jnp.where(odd_lane, col_r[k, 1, chunk], col_r[k, 0, chunk])
            for c in range(4):
                for u in range(CHUNK):
                    at = c * CHUNK + u
                    edge_ref[c, u] = pltpu.roll(beside, lanes - 1 - 2 * at, 1)
            for u in range(CHUNK):
                t = chunk * CHUNK + u
                if u < CHUNK - 1:
                    xp = load(t + 1)
                else:
                    ended = t == ct - 1
                    xp = load(jnp.minimum(t + 1, ct - 1))
                    xp = [jnp.where(ended, beyond[c], xp[c]) for c in range(4)]
                c_up, c_dn, c_lo, c_hi = wr_up[t], wr_dn[t], wa_lo[t], wa_hi[t]
                c_be, c_ah = wt[t], wt[t + 1]
                nb = []
                for c in range(4):
                    up, dn, lo, hi = around(
                        x[c], row_r[k, 0, c // 2, c % 2, t], row_r[k, 1, c // 2, c % 2, t], edge_ref[c, u]
                    )
                    nb.append(
                        (c_dn * dn + c_up * up)
                        + (c_hi * hi + c_lo * lo)
                        + (c_ah * xp[c] + c_be * xm[c])
                    )
                nb = lossy(nb)
                d_im = di[t]
                for h in range(2):
                    d_re = dr[h, t]
                    re, im = h, 2 + h
                    val_re = rhs_ref[0, h, t] - (d_re * x[re] - d_im * x[im] - nb[re])
                    val_im = rhs_ref[1, h, t] - (d_re * x[im] + d_im * x[re] - nb[im])
                    val_ref[0, h, t] = val_re
                    val_ref[1, h, t] = val_im
                    sums[re] = sums[re] + val_re
                    sums[im] = sums[im] + val_im
                xm, x = x, xp
            return tuple(xm) + tuple(x) + tuple(sums)

        def one_part(part, carry):
            on_faces(lambda d: halo_copy(k, part, d ^ 1).wait_recv())
            return lax.fori_loop(
                0, part_chunks, lambda n, carry: chunk_pass(part * part_chunks + n, carry), carry
            )

        return lax.fori_loop(0, PARTS, one_part, tuple(before) + tuple(start) + (zero,) * 4)[8:]

    for k in range(ITERS):
        final = k == ITERS - 1
        sums = apply_operator(k)
        coarse = finish_coarse(k)
        corr = [coarse[c * per : c * per + rows, 0:lanes] for c in range(4)]
        apart = [[], [], [], []]
        for c in range(4):
            line = c * per + rows
            beside = coarse[c * per : c * per + rows, lanes : 2 * lanes]
            shifted = (
                jnp.where(row == 0, coarse[line : line + 1, 0:lanes], pltpu.roll(corr[c], 1, 0)),
                jnp.where(
                    row == rows - 1,
                    coarse[line + 1 : line + 2, 0:lanes],
                    pltpu.roll(corr[c], rows - 1, 0),
                ),
                jnp.where(lane == 0, beside, pltpu.roll(corr[c], 1, 1)),
                jnp.where(
                    lane == lanes - 1,
                    pltpu.roll(beside, lanes - 2, 1),
                    pltpu.roll(corr[c], lanes - 1, 1),
                ),
            )
            for n in range(4):
                apart[n].append(corr[c] - shifted[n])
        push = [lossy(apart[n]) for n in range(4)]
        push.append([mass[c % 2] * corr[c] for c in range(4)])
        ends = []
        for sign, weight in ((-1.0, wt[0]), (1.0, wt[ct])):
            over = turn(trig, corr, sign)
            ends.append([weight * x for x in lossy([corr[c] - over[c] for c in range(4)])])
        if not final:
            restrict_and_send(
                k + 1,
                [
                    sums[c] - coarse_change(moved, push, c) - ends[0][c] - ends[1][c]
                    for c in range(4)
                ],
            )
        for c in range(4):
            val_ref[c // 2, c % 2, 0] = val_ref[c // 2, c % 2, 0] - ends[0][c]
            val_ref[c // 2, c % 2, ct - 1] = val_ref[c // 2, c % 2, ct - 1] - ends[1][c]
        if final:
            for c in range(4):
                corr_ref[c] = corr[c]
                for n in range(5):
                    push_ref[n, c] = push[n][c]
            break

        @pl.loop(0, PARTS)
        def _(part):
            on_faces(lambda d: halo_copy(k, part, d).wait_send())

        def update_chunk(chunk, nothing):
            packed = zero
            for u in range(CHUNK):
                t = chunk * CHUNK + u
                weights = (wr_up[t], wr_dn[t], wa_lo[t], wa_hi[t], dens[t])
                res = [
                    val_ref[c // 2, c % 2, t] - coarse_change(weights, push, c) for c in range(4)
                ]
                x = load(t)
                y = [None] * 4
                for h in range(2):
                    a, b = smooth(t, res[h], res[2 + h], h)
                    y[h], y[2 + h] = (x[h] + corr[h]) + a, (x[2 + h] + corr[2 + h]) + b
                for c in range(4):
                    sol_ref[c // 2, c % 2, t] = y[c]
                    packed = pack(y[c], c * CHUNK + u, packed)
            col_s[k + 1, chunk] = packed
            return nothing

        in_parts(k + 1, update_chunk, 0)

    on_faces(lambda d: stiff_copy(d).wait_send())

    @pl.loop(0, PARTS)
    def _(part):
        on_faces(lambda d: halo_copy(ITERS - 1, part, d).wait_send())

    for k in range(ITERS):

        @pl.loop(1, ndev)
        def _(d):
            gather(k, d).wait_send()


def last_pass(
    sol_ref,
    val_ref,
    wr_up,
    wr_dn,
    wa_lo,
    wa_hi,
    dens,
    corr_ref,
    push_ref,
    sol_hbm,
    res_hbm,
    sol_out,
    res_out,
    sem,
):
    ct = sol_ref.shape[2]
    chunks = ct // CHUNK
    corr = [corr_ref[c] for c in range(4)]
    push = [[push_ref[n, c] for c in range(4)] for n in range(5)]

    def put(n, chunk):
        src, dst = ((sol_out, sol_hbm), (res_out, res_hbm))[n]
        at = pl.ds(chunk * CHUNK, CHUNK)
        return pltpu.make_async_copy(src.at[:, :, at], dst.at[:, :, at], sem.at[n, chunk])

    @pl.loop(0, chunks)
    def _(chunk):
        for u in range(CHUNK):
            t = chunk * CHUNK + u
            weights = (wr_up[t], wr_dn[t], wa_lo[t], wa_hi[t], dens[t])
            for c in range(4):
                sol_out[c // 2, c % 2, t] = sol_ref[c // 2, c % 2, t] + corr[c]
                res_out[c // 2, c % 2, t] = val_ref[c // 2, c % 2, t] - coarse_change(
                    weights, push, c
                )
        for n in range(2):
            put(n, chunk).start()

    @pl.loop(0, chunks)
    def _(chunk):
        for n in range(2):
            put(n, chunk).wait()


def local(rhs, mat_ids, stiff_table, dens_table, mass_shift, harmonic, radial_factor, axial_factor):
    nrad = lax.axis_size("radial")
    nax = lax.axis_size("axial")
    ct, rows, lanes = mat_ids.shape
    vmem = pl.BlockSpec(memory_space=pltpu.VMEM)
    hbm = pl.BlockSpec(memory_space=pltpu.HBM)
    f32 = jnp.float32
    field = (ct, rows, lanes)
    chunks = ct // CHUNK
    groups = ct // GROUP
    cdev = 4 * (rows // AR)
    ndev = nrad * nax
    dma = pltpu.SemaphoreType.DMA
    inputs = (
        rhs,
        mat_ids,
        stiff_table,
        dens_table,
        mass_shift,
        harmonic,
        radial_factor,
        axial_factor,
    )
    held = (
        rhs.shape,
        rhs.shape,
        field,
        field,
        field,
        field,
        field,
        (4, rows, lanes),
        (5, 4, rows, lanes),
    )
    state = pl.pallas_call(
        functools.partial(kernel, nrad, nax),
        out_shape=tuple(pltpu.VMEM(shape, f32) for shape in held),
        in_specs=[hbm] * 8,
        out_specs=(vmem,) * len(held),
        scratch_shapes=[
            pltpu.VMEM(rhs.shape, f32),
            pltpu.VMEM(field, jnp.int32),
            pltpu.SMEM(stiff_table.shape, f32),
            pltpu.SMEM(dens_table.shape, f32),
            pltpu.SMEM(mass_shift.shape, f32),
            pltpu.SMEM(harmonic.shape, jnp.int32),
            pltpu.VMEM(radial_factor.shape, f32),
            pltpu.VMEM(axial_factor.shape, f32),
            dma((8,)),
            pltpu.VMEM((ct + 2, rows, lanes), f32),
            pltpu.VMEM((ct + 1, rows, lanes), f32),
            pltpu.VMEM((2,) + field, f32),
            pltpu.VMEM(field, f32),
            pltpu.VMEM((2,) + field, f32),
            pltpu.VMEM((4, CHUNK, rows, lanes), f32),
            pltpu.VMEM((2, ct, lanes), f32),
            pltpu.VMEM((2, ct, lanes), f32),
            pltpu.VMEM((groups, rows, lanes), f32),
            pltpu.VMEM((2, groups, rows, lanes), f32),
            pltpu.VMEM((chunks, rows, lanes), f32),
            pltpu.VMEM((ITERS, 2, 2, 2, ct, 1, lanes), f32),
            pltpu.VMEM((ITERS, chunks, rows, lanes), f32),
            pltpu.VMEM((ITERS, 2, chunks, rows, lanes), f32),
            pltpu.VMEM((ITERS, ndev, 1, lanes), f32),
            pltpu.VMEM((2, 3 * lanes, lanes), f32),
            pltpu.VMEM((8 * rows, 2 * nrad * cdev), f32),
            dma((4,)),
            dma((4,)),
            dma((ITERS, PARTS, 4)),
            dma((ITERS, PARTS, 4)),
            dma((ITERS, ndev)),
            dma((ITERS, ndev)),
        ],
        compiler_params=pltpu.CompilerParams(
            collective_id=0, has_side_effects=True, vmem_limit_bytes=48 * 1024 * 1024
        ),
    )(*[pltpu.with_memory_space_constraint(x, pltpu.HBM) for x in inputs])
    return pl.pallas_call(
        last_pass,
        out_shape=(jax.ShapeDtypeStruct(rhs.shape, f32), jax.ShapeDtypeStruct(rhs.shape, f32)),
        in_specs=[vmem] * len(held),
        out_specs=(hbm, hbm),
        scratch_shapes=[
            pltpu.VMEM(rhs.shape, f32),
            pltpu.VMEM(rhs.shape, f32),
            dma((2, chunks)),
        ],
        compiler_params=pltpu.CompilerParams(vmem_limit_bytes=32 * 1024 * 1024),
    )(*[pltpu.with_memory_space_constraint(x, pltpu.VMEM) for x in state])


def solution(mesh):
    return jax.shard_map(
        local,
        mesh=mesh,
        in_specs=(
            P(None, None, None, "radial", "axial"),
            P(None, "radial", "axial"),
            P(),
            P(),
            P(),
            P(),
            P(),
            P(),
        ),
        out_specs=(P(None, None, None, "radial", "axial"), P(None, None, None, "radial", "axial")),
        check_vma=False,
    )
```

```python
import functools

import jax
import jax.numpy as jnp
from jax import lax
from jax.experimental import pallas as pl
from jax.experimental.pallas import tpu as pltpu
from jax.sharding import PartitionSpec as P

ITERS = 3
NSECT = 24
AR = 4
AA = 8
LOSS_FACTOR = 0.2
RELAXATION = 0.6
MESH = pl.DeviceIdType.MESH
HIGHEST = lax.Precision.HIGHEST
CHUNK = 8
PARTS = 4
GROUP = 32


def dot(a, b):
    return jnp.dot(a, b, precision=HIGHEST, preferred_element_type=jnp.float32)


def grid_of(rows, lanes):
    return (
        lax.broadcasted_iota(jnp.int32, (rows, lanes), 0),
        lax.broadcasted_iota(jnp.int32, (rows, lanes), 1),
    )


def around(value, up, dn, edge):
    rows, lanes = value.shape
    row, lane = grid_of(rows, lanes)
    return (
        jnp.where(row == 0, up, pltpu.roll(value, 1, 0)),
        jnp.where(row == rows - 1, dn, pltpu.roll(value, rows - 1, 0)),
        pltpu.roll(jnp.where(lane == lanes - 1, edge, value), 1, 1),
        pltpu.roll(jnp.where(lane == 0, edge, value), lanes - 1, 1),
    )


def face_terms(fix_rows, fix_cols, t, chunk, c, u):
    rows, lanes = fix_cols.shape[1:]
    row, lane = grid_of(rows, lanes)
    edge = pltpu.roll(fix_cols[chunk], lanes - 1 - 2 * (c * CHUNK + u), 1)
    along = jnp.where(
        row == 0,
        fix_rows[0, c, pl.ds(t, 1), :],
        jnp.where(row == rows - 1, fix_rows[1, c, pl.ds(t, 1), :], 0.0),
    )
    return along + jnp.where((lane == 0) | (lane == lanes - 1), edge, 0.0)


def lossy(x):
    return [x[h] - LOSS_FACTOR * x[2 + h] for h in range(2)] + [
        x[2 + h] + LOSS_FACTOR * x[h] for h in range(2)
    ]


def coarse_change(weights, push, c):
    w_up, w_dn, w_lo, w_hi, dens = weights
    return ((w_up * push[0][c] + w_dn * push[1][c]) + (w_lo * push[2][c] + w_hi * push[3][c])) - (
        dens * push[4][c]
    )


def turn(trig, x, sign):
    cosines, sines = trig[0:2], trig[2:4]
    return [cosines[h] * x[h] - sign * sines[h] * x[2 + h] for h in range(2)] + [
        sign * sines[h] * x[h] + cosines[h] * x[2 + h] for h in range(2)
    ]


def kernel(
    nrad,
    nax,
    rhs_hbm,
    ids_hbm,
    stiff_hbm,
    dens_hbm,
    mass_hbm,
    harm_hbm,
    radial_hbm,
    axial_hbm,
    sol_ref,
    val_ref,
    wr_up,
    wr_dn,
    wa_lo,
    wa_hi,
    dens,
    corr_ref,
    push_ref,
    fix_rows,
    fix_cols,
    rhs_ref,
    ids_ref,
    stiff_ref,
    dens_ref,
    mass_ref,
    harm_ref,
    radial_ref,
    axial_ref,
    in_sem,
    stiff,
    wt,
    dr,
    di,
    sc,
    w_rows,
    w_cols,
    srow_s,
    srow_r,
    scol_s,
    scol_r,
    scol_m,
    row_r,
    col_s,
    col_r,
    all_r,
    axmat,
    radmat,
    st_send,
    st_recv,
    ha_send,
    ha_recv,
    ga_send,
    ga_recv,
):
    loads = [
        pltpu.make_async_copy(src, dst, in_sem.at[n])
        for n, (src, dst) in enumerate(
            (
                (stiff_hbm, stiff_ref),
                (ids_hbm, ids_ref),
                (rhs_hbm, rhs_ref),
                (dens_hbm, dens_ref),
                (mass_hbm, mass_ref),
                (harm_hbm, harm_ref),
                (radial_hbm, radial_ref),
                (axial_hbm, axial_ref),
            )
        )
    ]
    for load_in in loads:
        load_in.start()
    ct = rhs_ref.shape[2]
    rows, lanes = rhs_ref.shape[3:]
    gr = radial_ref.shape[2]
    ga = axial_ref.shape[2]
    band_r = rows // AR
    band_c = lanes // AA
    chunks = ct // CHUNK
    ndev = nrad * nax
    i = lax.axis_index("radial")
    j = lax.axis_index("axial")
    me = i * nax + j
    has_up, has_dn = i > 0, i < nrad - 1
    has_lo, has_hi = j > 0, j < nax - 1
    conds = (has_up, has_dn, has_lo, has_hi)
    targets = ({"radial": i - 1}, {"radial": i + 1}, {"axial": j - 1}, {"axial": j + 1})

    def peer(d):
        at = lax.rem(me + d, ndev)
        return {"radial": at // nax, "axial": lax.rem(at, nax)}

    barrier = pltpu.get_barrier_semaphore()

    @pl.loop(1, ndev)
    def _(d):
        pl.semaphore_signal(barrier, inc=1, device_id=peer(d), device_id_type=MESH)

    for d in range(4):

        @pl.when(jnp.logical_not(conds[d]))
        def _():
            if d < 2:
                srow_r[d] = jnp.zeros(srow_r.shape[1:], jnp.float32)
                for k in range(ITERS):
                    row_r[k, d] = jnp.zeros(row_r.shape[2:], jnp.float32)
            else:
                scol_r[d - 2] = jnp.zeros(scol_r.shape[1:], jnp.float32)
                for k in range(ITERS):
                    col_r[k, d - 2] = jnp.zeros(col_r.shape[2:], jnp.float32)

    row, lane = grid_of(rows, lanes)
    zero = jnp.zeros((rows, lanes), jnp.float32)
    pair = lane // 2
    odd_lane = lane % 2 == 1

    def lookup(ids, table):
        value = jnp.full(ids.shape, table[0], jnp.float32)
        for entry in range(1, table.shape[0]):
            value = jnp.where(ids == entry, table[entry], value)
        return value

    def pack(value, at, packed):
        return jnp.where(pair == at, pltpu.roll(value, (2 * at + 1) % lanes, 1), packed)

    def stiff_copy(d):
        if d < 2:
            src, dst = srow_s.at[d], srow_r.at[1 - d]
        else:
            src, dst = scol_s, scol_r.at[3 - d]
        return pltpu.make_async_remote_copy(
            src_ref=src,
            dst_ref=dst,
            send_sem=st_send.at[d],
            recv_sem=st_recv.at[d ^ 1],
            device_id=targets[d],
            device_id_type=MESH,
        )

    part_chunks = chunks // PARTS
    part_ct = ct // PARTS

    def halo_copy(k, part, d):
        if d < 2:
            at = pl.ds(part * part_ct, part_ct)
            line = 0 if d == 0 else rows - 1
            src, dst = sol_ref.at[:, :, at, line], row_r.at[k, 1 - d, :, :, at]
        else:
            at = pl.ds(part * part_chunks, part_chunks)
            src, dst = col_s.at[k, at], col_r.at[k, 3 - d, at]
        return pltpu.make_async_remote_copy(
            src_ref=src,
            dst_ref=dst,
            send_sem=ha_send.at[k, part, d],
            recv_sem=ha_recv.at[k, part, d ^ 1],
            device_id=targets[d],
            device_id_type=MESH,
        )

    def gather(k, d):
        return pltpu.make_async_remote_copy(
            src_ref=all_r.at[k, me],
            dst_ref=all_r.at[k, me],
            send_sem=ga_send.at[k, d],
            recv_sem=ga_recv.at[k, d],
            device_id=peer(d),
            device_id_type=MESH,
        )

    def on_faces(act):
        for d in range(4):

            @pl.when(conds[d])
            def _():
                act(d)

    loads[0].wait()
    loads[1].wait()

    @pl.loop(0, ct // GROUP)
    def _(group):
        packed = zero
        for u in range(GROUP):
            t = group * GROUP + u
            value = lookup(ids_ref[t], stiff_ref)
            stiff[t + 1] = value
            srow_s[0, pl.ds(t, 1), :] = value[0:1]
            srow_s[1, pl.ds(t, 1), :] = value[rows - 1 : rows]
            packed = pack(value, u, packed)
        scol_s[group] = packed

    stiff[0] = stiff[ct]
    stiff[ct + 1] = stiff[1]

    pl.semaphore_wait(barrier, ndev - 1)
    on_faces(lambda d: stiff_copy(d).start())

    e_row, e_col = grid_of(lanes, lanes)
    fold = jnp.where(e_row // AA == e_col % band_c, 1.0, 0.0)
    k_row, k_col = grid_of(4 * rows, lanes)
    keep = k_row // AR == (j + rows - k_col // band_c) % rows

    def restrict_and_send(k, sums):
        folded = dot(jnp.concatenate(sums, axis=0), fold)
        all_r[k, me] = jnp.sum(jnp.where(keep, folded, 0.0), axis=0, keepdims=True)

        @pl.loop(1, ndev)
        def _(d):
            gather(k, d).start()

    loads[2].wait()

    def sum_pass(chunk, sums):
        sums = list(sums)
        for u in range(CHUNK):
            for c in range(4):
                sums[c] = sums[c] + rhs_ref[c // 2, c % 2, chunk * CHUNK + u]
        return tuple(sums)

    restrict_and_send(0, lax.fori_loop(0, chunks, sum_pass, (zero,) * 4))
    for load_in in loads[3:]:
        load_in.wait()

    ax_row, ax_col = grid_of(lanes, ga)
    own = jnp.where(ax_row // AA + j * band_c == ax_col, 1.0, 0.0)
    half = lanes // 2
    side = jnp.where(ax_row % 2 == 0, j * band_c - 1, (j + 1) * band_c) == ax_col
    edges = [jnp.where(side & (ax_row // half == p), 1.0, 0.0) for p in range(2)]
    for h in range(2):
        if ga < lanes:
            axmat[h] = jnp.zeros(axmat.shape[1:], jnp.float32)
        axmat[h, 0:lanes, 0:ga] = dot(own, axial_ref[0, h])
        axmat[h, lanes : 2 * lanes, 0:ga] = dot(own, axial_ref[1, h])
        axmat[h, 2 * lanes : 3 * lanes, 0:ga] = dot(edges[0], axial_ref[0, h]) + dot(
            edges[1], axial_ref[1, h]
        )

    per = 2 * rows
    cdev = 4 * band_r
    r_row, r_col = grid_of(4 * per, gr)
    r_row = r_row % per
    want = jnp.where(
        r_row < rows,
        r_row // AR + i * band_r,
        jnp.where(
            r_row == rows, i * band_r - 1, jnp.where(r_row == rows + 1, (i + 1) * band_r, -1)
        ),
    )
    r_sel = jnp.where(want == r_col, 1.0, 0.0)
    c_row, c_col = grid_of(gr, nrad * cdev)
    c_sel = jnp.where((c_col // cdev) * band_r + c_col % band_r == c_row, 1.0, 0.0)
    m_row, m_col = grid_of(4 * per, nrad * cdev)
    m_out = m_row // per
    m_in = (m_col % cdev) // band_r
    first = jnp.zeros((4 * per, nrad * cdev), jnp.float32)
    second = first
    for h in range(2):
        same = (m_out == m_in) & (m_out % 2 == h)
        to_re = (m_out == h) & (m_in == 2 + h)
        to_im = (m_out == 2 + h) & (m_in == h)
        real = dot(dot(r_sel, radial_ref[0, h]), c_sel)
        imag = dot(dot(r_sel, radial_ref[1, h]), c_sel)
        first = jnp.where(same, real, first)
        first = jnp.where(to_re, -imag, first)
        first = jnp.where(to_im, imag, first)
        second = jnp.where(same, -imag, second)
        second = jnp.where(to_re, -real, second)
        second = jnp.where(to_im, real, second)
    radmat[:, 0 : nrad * cdev] = first
    radmat[:, nrad * cdev : 2 * nrad * cdev] = second

    p_row, _ = grid_of(nrad * cdev, 3 * lanes)
    odd_harm = (p_row // band_r) % 2 == 1

    def finish_coarse(k):
        @pl.loop(1, ndev)
        def _(d):
            gather(k, d).wait_recv()

        tiles = []
        for a in range(nrad):
            tile = zero
            for b in range(nax):
                tile = jnp.where((lane // band_c + row) % rows == b, all_r[k, a * nax + b], tile)
            tile = pltpu.roll(tile, 0, 1, stride=band_c, stride_axis=0)
            tiles.append(tile)
        whole = jnp.concatenate(tiles, axis=0)
        prod = [
            lax.dot_general(
                whole,
                axmat[h],
                (((1,), (1,)), ((), ())),
                precision=HIGHEST,
                preferred_element_type=jnp.float32,
            )
            for h in range(2)
        ]
        prod = jnp.where(odd_harm, prod[1], prod[0])
        a = prod[:, 0:lanes]
        b = prod[:, lanes : 2 * lanes]
        e = prod[:, 2 * lanes : 3 * lanes]
        f = pltpu.roll(e, half, 1)
        mixed = jnp.concatenate(
            [jnp.concatenate([a, e], axis=1), jnp.concatenate([b, f], axis=1)], axis=0
        )
        return dot(radmat[...], mixed)

    on_faces(lambda d: stiff_copy(d ^ 1).wait_recv())

    mass = [mass_ref[0], mass_ref[1]]

    def smooth(t, rr, ri, h):
        d_re, d_im, scale = dr[h, t], di[t], sc[h, t]
        return (d_re * rr + d_im * ri) * scale, (d_re * ri - d_im * rr) * scale

    per_group = GROUP // CHUNK
    for n in range(ct // GROUP):
        merged = jnp.where(odd_lane, scol_r[1, n], scol_r[0, n])
        for m in range(per_group):
            scol_m[n * per_group + m] = (
                merged if m == 0 else pltpu.roll(merged, lanes - 2 * CHUNK * m, 1)
            )

    def setup_step(t, u, packed, faces, beside, moved):
        value = stiff[t + 1]
        up, dn, lo, hi = around(
            value,
            srow_r[0, pl.ds(t, 1), :],
            srow_r[1, pl.ds(t, 1), :],
            pltpu.roll(beside, lanes - 1 - 2 * u, 1),
        )
        c_up, c_dn = 0.5 * (value + up), 0.5 * (value + dn)
        c_lo, c_hi = 0.5 * (value + lo), 0.5 * (value + hi)
        c_be, c_ah = 0.5 * (value + stiff[t]), 0.5 * (value + stiff[t + 2])
        wr_up[t] = c_up
        wr_dn[t] = c_dn
        wa_lo[t] = c_lo
        wa_hi[t] = c_hi
        w_rows[0, pl.ds(t, 1), :] = c_up[0:1]
        w_rows[1, pl.ds(t, 1), :] = c_dn[rows - 1 : rows]
        wt[t] = c_be
        wt[t + 1] = c_ah
        total = c_dn + c_up + c_hi + c_lo + c_ah + c_be
        density = lookup(ids_ref[t], dens_ref)
        dens[t] = density
        moved = [m + w for m, w in zip(moved, (c_up, c_dn, c_lo, c_hi, density))]
        d_im = LOSS_FACTOR * total
        di[t] = d_im
        y = [None] * 4
        for h in range(2):
            d_re = total - mass[h] * density
            scale = RELAXATION / (d_re * d_re + d_im * d_im)
            dr[h, t] = d_re
            sc[h, t] = scale
            rr, ri = rhs_ref[0, h, t], rhs_ref[1, h, t]
            y[h] = (d_re * rr + d_im * ri) * scale
            y[2 + h] = (d_re * ri - d_im * rr) * scale
            sol_ref[0, h, t] = y[h]
            sol_ref[1, h, t] = y[2 + h]
        for c in range(4):
            packed = pack(y[c], c * CHUNK + u, packed)
        faces = pack(jnp.where(lane == 0, c_lo, c_hi), u, faces)
        return packed, faces, moved

    def in_parts(k, step, carry):
        def one_part(part, carry):
            carry = lax.fori_loop(
                0,
                part_chunks,
                lambda n, carry: step(part * part_chunks + n, carry),
                carry,
                unroll=True,
            )
            on_faces(lambda d: halo_copy(k, part, d).start())
            return carry

        return lax.fori_loop(0, PARTS, one_part, carry)

    def setup_chunk(chunk, moved):
        packed = zero
        faces = zero
        beside = scol_m[chunk]
        for u in range(CHUNK):
            packed, faces, moved = setup_step(chunk * CHUNK + u, u, packed, faces, beside, moved)
        col_s[0, chunk] = packed
        faces = faces + pltpu.roll(faces, 2 * CHUNK, 1)
        w_cols[chunk] = faces + pltpu.roll(faces, 4 * CHUNK, 1)
        return tuple(moved)

    moved = in_parts(0, setup_chunk, (zero,) * 5)

    trig = [[], []]
    for h in range(2):
        angle = jnp.full((rows, lanes), harm_ref[h], jnp.int32).astype(jnp.float32) * (
            2.0 * jnp.pi / NSECT
        )
        trig[0].append(jnp.cos(angle))
        trig[1].append(jnp.sin(angle))
    trig = trig[0] + trig[1]

    def load(t):
        return [sol_ref[c // 2, c % 2, t] for c in range(4)]

    def apply_operator(k):
        start = load(0)
        beyond = turn(trig, start, 1.0)
        before = turn(trig, load(ct - 1), -1.0)

        def chunk_pass(chunk, carry):
            xm, x, sums = list(carry[0:4]), list(carry[4:8]), list(carry[8:])
            for u in range(CHUNK):
                t = chunk * CHUNK + u
                if u < CHUNK - 1:
                    xp = load(t + 1)
                else:
                    ended = t == ct - 1
                    xp = load(jnp.minimum(t + 1, ct - 1))
                    xp = [jnp.where(ended, beyond[c], xp[c]) for c in range(4)]
                c_up, c_dn, c_lo, c_hi = wr_up[t], wr_dn[t], wa_lo[t], wa_hi[t]
                c_be, c_ah = wt[t], wt[t + 1]
                nb = []
                for c in range(4):
                    up = jnp.where(row == 0, 0.0, pltpu.roll(x[c], 1, 0))
                    dn = jnp.where(row == rows - 1, 0.0, pltpu.roll(x[c], rows - 1, 0))
                    lo = jnp.where(lane == 0, 0.0, pltpu.roll(x[c], 1, 1))
                    hi = jnp.where(lane == lanes - 1, 0.0, pltpu.roll(x[c], lanes - 1, 1))
                    nb.append(
                        (c_dn * dn + c_up * up)
                        + (c_hi * hi + c_lo * lo)
                        + (c_ah * xp[c] + c_be * xm[c])
                    )
                nb = lossy(nb)
                d_im = di[t]
                for h in range(2):
                    d_re = dr[h, t]
                    re, im = h, 2 + h
                    val_re = rhs_ref[0, h, t] - (d_re * x[re] - d_im * x[im] - nb[re])
                    val_im = rhs_ref[1, h, t] - (d_re * x[im] + d_im * x[re] - nb[im])
                    val_ref[0, h, t] = val_re
                    val_ref[1, h, t] = val_im
                    sums[re] = sums[re] + val_re
                    sums[im] = sums[im] + val_im
                xm, x = x, xp
            return tuple(xm) + tuple(x) + tuple(sums)

        carry = tuple(before) + tuple(start) + (zero,) * 4
        return lax.fori_loop(0, chunks, chunk_pass, carry, unroll=4)[8:]

    def fix_faces(k, sums):
        @pl.loop(0, PARTS)
        def _(part):
            on_faces(lambda d: halo_copy(k, part, d ^ 1).wait_recv())

        def chunk_fix(chunk, carry):
            out = []
            at = pl.ds(pl.multiple_of(chunk * CHUNK, CHUNK), CHUNK)
            for side in range(2):
                weight = w_rows[side, at]
                term = lossy([weight * row_r[k, side, c // 2, c % 2, at] for c in range(4)])
                for c in range(4):
                    fix_rows[side, c, at] = term[c]
                    out.append(carry[4 * side + c] + term[c])
            term = w_cols[chunk] * jnp.where(
                odd_lane,
                pltpu.roll(col_r[k, 0, chunk], 1, 1),
                pltpu.roll(col_r[k, 1, chunk], lanes - 1, 1),
            )
            turned = jnp.where(
                pair < 2 * CHUNK,
                -pltpu.roll(term, lanes - 4 * CHUNK, 1),
                pltpu.roll(term, 4 * CHUNK, 1),
            )
            term = term + LOSS_FACTOR * turned
            fix_cols[chunk] = term
            return tuple(out) + (carry[8] + term,)

        carry = lax.fori_loop(0, chunks, chunk_fix, (zero,) * 9, unroll=4)
        beside = carry[8]
        step = 1
        while step < CHUNK:
            beside = beside + pltpu.roll(beside, lanes - 2 * step, 1)
            step *= 2
        outs = []
        for c in range(4):
            edge = pltpu.roll(beside, lanes - 1 - 2 * c * CHUNK, 1)
            outs.append(
                sums[c]
                + jnp.where(row == 0, jnp.sum(carry[c], axis=0, keepdims=True), 0.0)
                + jnp.where(row == rows - 1, jnp.sum(carry[4 + c], axis=0, keepdims=True), 0.0)
                + jnp.where((lane == 0) | (lane == lanes - 1), edge, 0.0)
            )
        return outs

    for k in range(ITERS):
        final = k == ITERS - 1
        sums = apply_operator(k)
        coarse = finish_coarse(k)
        corr = [coarse[c * per : c * per + rows, 0:lanes] for c in range(4)]
        apart = [[], [], [], []]
        for c in range(4):
            line = c * per + rows
            beside = coarse[c * per : c * per + rows, lanes : 2 * lanes]
            shifted = (
                jnp.where(row == 0, coarse[line : line + 1, 0:lanes], pltpu.roll(corr[c], 1, 0)),
                jnp.where(
                    row == rows - 1,
                    coarse[line + 1 : line + 2, 0:lanes],
                    pltpu.roll(corr[c], rows - 1, 0),
                ),
                jnp.where(lane == 0, beside, pltpu.roll(corr[c], 1, 1)),
                jnp.where(
                    lane == lanes - 1,
                    pltpu.roll(beside, lanes - 2, 1),
                    pltpu.roll(corr[c], lanes - 1, 1),
                ),
            )
            for n in range(4):
                apart[n].append(corr[c] - shifted[n])
        push = [lossy(apart[n]) for n in range(4)]
        push.append([mass[c % 2] * corr[c] for c in range(4)])
        ends = []
        for sign, weight in ((-1.0, wt[0]), (1.0, wt[ct])):
            over = turn(trig, corr, sign)
            ends.append([weight * x for x in lossy([corr[c] - over[c] for c in range(4)])])
        sums = fix_faces(k, sums)
        if not final:
            restrict_and_send(
                k + 1,
                [
                    sums[c] - coarse_change(moved, push, c) - ends[0][c] - ends[1][c]
                    for c in range(4)
                ],
            )
        for c in range(4):
            val_ref[c // 2, c % 2, 0] = val_ref[c // 2, c % 2, 0] - ends[0][c]
            val_ref[c // 2, c % 2, ct - 1] = val_ref[c // 2, c % 2, ct - 1] - ends[1][c]
        if final:
            for c in range(4):
                corr_ref[c] = corr[c]
                for n in range(5):
                    push_ref[n, c] = push[n][c]
            break

        @pl.loop(0, PARTS)
        def _(part):
            on_faces(lambda d: halo_copy(k, part, d).wait_send())

        def update_chunk(chunk, nothing):
            packed = zero
            for u in range(CHUNK):
                t = chunk * CHUNK + u
                weights = (wr_up[t], wr_dn[t], wa_lo[t], wa_hi[t], dens[t])
                res = [
                    (val_ref[c // 2, c % 2, t] - coarse_change(weights, push, c))
                    + face_terms(fix_rows, fix_cols, t, chunk, c, u)
                    for c in range(4)
                ]
                x = load(t)
                y = [None] * 4
                for h in range(2):
                    a, b = smooth(t, res[h], res[2 + h], h)
                    y[h], y[2 + h] = (x[h] + corr[h]) + a, (x[2 + h] + corr[2 + h]) + b
                for c in range(4):
                    sol_ref[c // 2, c % 2, t] = y[c]
                    packed = pack(y[c], c * CHUNK + u, packed)
            col_s[k + 1, chunk] = packed
            return nothing

        in_parts(k + 1, update_chunk, 0)

    on_faces(lambda d: stiff_copy(d).wait_send())

    @pl.loop(0, PARTS)
    def _(part):
        on_faces(lambda d: halo_copy(ITERS - 1, part, d).wait_send())

    for k in range(ITERS):

        @pl.loop(1, ndev)
        def _(d):
            gather(k, d).wait_send()


def last_pass(
    sol_ref,
    val_ref,
    wr_up,
    wr_dn,
    wa_lo,
    wa_hi,
    dens,
    corr_ref,
    push_ref,
    fix_rows,
    fix_cols,
    sol_hbm,
    res_hbm,
    sol_out,
    res_out,
    sem,
):
    ct = sol_ref.shape[2]
    chunks = ct // CHUNK
    corr = [corr_ref[c] for c in range(4)]
    push = [[push_ref[n, c] for c in range(4)] for n in range(5)]

    def put(n, chunk):
        src, dst = ((sol_out, sol_hbm), (res_out, res_hbm))[n]
        at = pl.ds(chunk * CHUNK, CHUNK)
        return pltpu.make_async_copy(src.at[:, :, at], dst.at[:, :, at], sem.at[n, chunk])

    @pl.loop(0, chunks)
    def _(chunk):
        for u in range(CHUNK):
            t = chunk * CHUNK + u
            weights = (wr_up[t], wr_dn[t], wa_lo[t], wa_hi[t], dens[t])
            for c in range(4):
                sol_out[c // 2, c % 2, t] = sol_ref[c // 2, c % 2, t] + corr[c]
                res_out[c // 2, c % 2, t] = (
                    val_ref[c // 2, c % 2, t] - coarse_change(weights, push, c)
                ) + face_terms(fix_rows, fix_cols, t, chunk, c, u)
        for n in range(2):
            put(n, chunk).start()

    @pl.loop(0, chunks)
    def _(chunk):
        for n in range(2):
            put(n, chunk).wait()


def local(rhs, mat_ids, stiff_table, dens_table, mass_shift, harmonic, radial_factor, axial_factor):
    nrad = lax.axis_size("radial")
    nax = lax.axis_size("axial")
    ct, rows, lanes = mat_ids.shape
    vmem = pl.BlockSpec(memory_space=pltpu.VMEM)
    hbm = pl.BlockSpec(memory_space=pltpu.HBM)
    f32 = jnp.float32
    field = (ct, rows, lanes)
    chunks = ct // CHUNK
    groups = ct // GROUP
    cdev = 4 * (rows // AR)
    ndev = nrad * nax
    dma = pltpu.SemaphoreType.DMA
    inputs = (
        rhs,
        mat_ids,
        stiff_table,
        dens_table,
        mass_shift,
        harmonic,
        radial_factor,
        axial_factor,
    )
    held = (
        rhs.shape,
        rhs.shape,
        field,
        field,
        field,
        field,
        field,
        (4, rows, lanes),
        (5, 4, rows, lanes),
        (2, 4, ct, lanes),
        (chunks, rows, lanes),
    )
    state = pl.pallas_call(
        functools.partial(kernel, nrad, nax),
        out_shape=tuple(pltpu.VMEM(shape, f32) for shape in held),
        in_specs=[hbm] * 8,
        out_specs=(vmem,) * len(held),
        scratch_shapes=[
            pltpu.VMEM(rhs.shape, f32),
            pltpu.VMEM(field, jnp.int32),
            pltpu.SMEM(stiff_table.shape, f32),
            pltpu.SMEM(dens_table.shape, f32),
            pltpu.SMEM(mass_shift.shape, f32),
            pltpu.SMEM(harmonic.shape, jnp.int32),
            pltpu.VMEM(radial_factor.shape, f32),
            pltpu.VMEM(axial_factor.shape, f32),
            dma((8,)),
            pltpu.VMEM((ct + 2, rows, lanes), f32),
            pltpu.VMEM((ct + 1, rows, lanes), f32),
            pltpu.VMEM((2,) + field, f32),
            pltpu.VMEM(field, f32),
            pltpu.VMEM((2,) + field, f32),
            pltpu.VMEM((2, ct, lanes), f32),
            pltpu.VMEM((chunks, rows, lanes), f32),
            pltpu.VMEM((2, ct, lanes), f32),
            pltpu.VMEM((2, ct, lanes), f32),
            pltpu.VMEM((groups, rows, lanes), f32),
            pltpu.VMEM((2, groups, rows, lanes), f32),
            pltpu.VMEM((chunks, rows, lanes), f32),
            pltpu.VMEM((ITERS, 2, 2, 2, ct, lanes), f32),
            pltpu.VMEM((ITERS, chunks, rows, lanes), f32),
            pltpu.VMEM((ITERS, 2, chunks, rows, lanes), f32),
            pltpu.VMEM((ITERS, ndev, 1, lanes), f32),
            pltpu.VMEM((2, 3 * lanes, lanes), f32),
            pltpu.VMEM((8 * rows, 2 * nrad * cdev), f32),
            dma((4,)),
            dma((4,)),
            dma((ITERS, PARTS, 4)),
            dma((ITERS, PARTS, 4)),
            dma((ITERS, ndev)),
            dma((ITERS, ndev)),
        ],
        compiler_params=pltpu.CompilerParams(
            collective_id=0, has_side_effects=True, vmem_limit_bytes=48 * 1024 * 1024
        ),
    )(*[pltpu.with_memory_space_constraint(x, pltpu.HBM) for x in inputs])
    return pl.pallas_call(
        last_pass,
        out_shape=(jax.ShapeDtypeStruct(rhs.shape, f32), jax.ShapeDtypeStruct(rhs.shape, f32)),
        in_specs=[vmem] * len(held),
        out_specs=(hbm, hbm),
        scratch_shapes=[
            pltpu.VMEM(rhs.shape, f32),
            pltpu.VMEM(rhs.shape, f32),
            dma((2, chunks)),
        ],
        compiler_params=pltpu.CompilerParams(vmem_limit_bytes=32 * 1024 * 1024),
    )(*[pltpu.with_memory_space_constraint(x, pltpu.VMEM) for x in state])


def solution(mesh):
    return jax.shard_map(
        local,
        mesh=mesh,
        in_specs=(
            P(None, None, None, "radial", "axial"),
            P(None, "radial", "axial"),
            P(),
            P(),
            P(),
            P(),
            P(),
            P(),
        ),
        out_specs=(P(None, None, None, "radial", "axial"), P(None, None, None, "radial", "axial")),
        check_vma=False,
    )
```

```python
import functools

import jax
import jax.numpy as jnp
from jax import lax
from jax.experimental import pallas as pl
from jax.experimental.pallas import tpu as pltpu
from jax.sharding import PartitionSpec as P

ITERS = 3
NSECT = 24
AR = 4
AA = 8
LOSS_FACTOR = 0.2
RELAXATION = 0.6
MESH = pl.DeviceIdType.MESH
HIGHEST = lax.Precision.HIGHEST
CHUNK = 8
PARTS = 4
GROUP = 32


def dot(a, b):
    return jnp.dot(a, b, precision=HIGHEST, preferred_element_type=jnp.float32)


def grid_of(rows, lanes):
    return (
        lax.broadcasted_iota(jnp.int32, (rows, lanes), 0),
        lax.broadcasted_iota(jnp.int32, (rows, lanes), 1),
    )


def around(value, up, dn, edge):
    rows, lanes = value.shape
    row, lane = grid_of(rows, lanes)
    return (
        jnp.where(row == 0, up, pltpu.roll(value, 1, 0)),
        jnp.where(row == rows - 1, dn, pltpu.roll(value, rows - 1, 0)),
        pltpu.roll(jnp.where(lane == lanes - 1, edge, value), 1, 1),
        pltpu.roll(jnp.where(lane == 0, edge, value), lanes - 1, 1),
    )


def face_terms(fix_rows, fix_cols, t, chunk, c, u):
    rows, lanes = fix_cols.shape[1:]
    row, lane = grid_of(rows, lanes)
    edge = pltpu.roll(fix_cols[chunk], lanes - 1 - 2 * (c * CHUNK + u), 1)
    along = jnp.where(
        row == 0,
        fix_rows[0, c, pl.ds(t, 1), :],
        jnp.where(row == rows - 1, fix_rows[1, c, pl.ds(t, 1), :], 0.0),
    )
    return along + jnp.where((lane == 0) | (lane == lanes - 1), edge, 0.0)


def lossy(x):
    return [x[h] - LOSS_FACTOR * x[2 + h] for h in range(2)] + [
        x[2 + h] + LOSS_FACTOR * x[h] for h in range(2)
    ]


def coarse_change(weights, push, c):
    w_up, w_dn, w_lo, w_hi, dens = weights
    return ((w_up * push[0][c] + w_dn * push[1][c]) + (w_lo * push[2][c] + w_hi * push[3][c])) - (
        dens * push[4][c]
    )


def turn(trig, x, sign):
    cosines, sines = trig[0:2], trig[2:4]
    return [cosines[h] * x[h] - sign * sines[h] * x[2 + h] for h in range(2)] + [
        sign * sines[h] * x[h] + cosines[h] * x[2 + h] for h in range(2)
    ]


def kernel(
    nrad,
    nax,
    rhs_hbm,
    ids_hbm,
    stiff_hbm,
    dens_hbm,
    mass_hbm,
    harm_hbm,
    radial_hbm,
    axial_hbm,
    sol_ref,
    val_ref,
    wr_up,
    wr_dn,
    wa_lo,
    wa_hi,
    dens,
    corr_ref,
    push_ref,
    fix_rows,
    fix_cols,
    rhs_ref,
    ids_ref,
    stiff_ref,
    dens_ref,
    mass_ref,
    harm_ref,
    radial_ref,
    axial_ref,
    in_sem,
    stiff,
    wt,
    dr,
    di,
    sc,
    w_rows,
    w_cols,
    srow_s,
    srow_r,
    scol_s,
    scol_r,
    scol_m,
    row_r,
    col_s,
    col_r,
    all_r,
    axmat,
    radmat,
    st_send,
    st_recv,
    ha_send,
    ha_recv,
    ga_send,
    ga_recv,
):
    loads = [
        pltpu.make_async_copy(src, dst, in_sem.at[n])
        for n, (src, dst) in enumerate(
            (
                (stiff_hbm, stiff_ref),
                (ids_hbm, ids_ref),
                (rhs_hbm, rhs_ref),
                (dens_hbm, dens_ref),
                (mass_hbm, mass_ref),
                (harm_hbm, harm_ref),
                (radial_hbm, radial_ref),
                (axial_hbm, axial_ref),
            )
        )
    ]
    for load_in in loads:
        load_in.start()
    ct = rhs_ref.shape[2]
    rows, lanes = rhs_ref.shape[3:]
    gr = radial_ref.shape[2]
    ga = axial_ref.shape[2]
    band_r = rows // AR
    band_c = lanes // AA
    chunks = ct // CHUNK
    ndev = nrad * nax
    i = lax.axis_index("radial")
    j = lax.axis_index("axial")
    me = i * nax + j
    has_up, has_dn = i > 0, i < nrad - 1
    has_lo, has_hi = j > 0, j < nax - 1
    conds = (has_up, has_dn, has_lo, has_hi)
    targets = ({"radial": i - 1}, {"radial": i + 1}, {"axial": j - 1}, {"axial": j + 1})

    def each_peer(act):
        def along(a):
            to = i + a
            to = jnp.where(to >= nrad, to - nrad, to)
            for b in range(nax):
                at = j + b
                act({"radial": to, "axial": jnp.where(at >= nax, at - nax, at)})

        for b in range(1, nax):
            at = j + b
            act({"radial": i, "axial": jnp.where(at >= nax, at - nax, at)})
        if nrad <= 8:
            for a in range(1, nrad):
                along(a)
        else:
            pl.loop(1, nrad)(along)

    barrier = pltpu.get_barrier_semaphore()
    each_peer(
        lambda peer: pl.semaphore_signal(barrier, inc=1, device_id=peer, device_id_type=MESH)
    )

    for d in range(4):

        @pl.when(jnp.logical_not(conds[d]))
        def _():
            if d < 2:
                srow_r[d] = jnp.zeros(srow_r.shape[1:], jnp.float32)
                for k in range(ITERS):
                    row_r[k, d] = jnp.zeros(row_r.shape[2:], jnp.float32)
            else:
                scol_r[d - 2] = jnp.zeros(scol_r.shape[1:], jnp.float32)
                for k in range(ITERS):
                    col_r[k, d - 2] = jnp.zeros(col_r.shape[2:], jnp.float32)

    row, lane = grid_of(rows, lanes)
    zero = jnp.zeros((rows, lanes), jnp.float32)
    pair = lane // 2
    odd_lane = lane % 2 == 1

    def lookup(ids, table):
        value = jnp.full(ids.shape, table[0], jnp.float32)
        for entry in range(1, table.shape[0]):
            value = jnp.where(ids == entry, table[entry], value)
        return value

    def pack(value, at, packed):
        return jnp.where(pair == at, pltpu.roll(value, (2 * at + 1) % lanes, 1), packed)

    def stiff_copy(d):
        if d < 2:
            src, dst = srow_s.at[d], srow_r.at[1 - d]
        else:
            src, dst = scol_s, scol_r.at[3 - d]
        return pltpu.make_async_remote_copy(
            src_ref=src,
            dst_ref=dst,
            send_sem=st_send.at[d],
            recv_sem=st_recv.at[d ^ 1],
            device_id=targets[d],
            device_id_type=MESH,
        )

    part_chunks = chunks // PARTS
    part_ct = ct // PARTS

    def halo_copy(k, part, d):
        if d < 2:
            at = pl.ds(part * part_ct, part_ct)
            line = 0 if d == 0 else rows - 1
            src, dst = sol_ref.at[:, :, at, line], row_r.at[k, 1 - d, :, :, at]
        else:
            at = pl.ds(part * part_chunks, part_chunks)
            src, dst = col_s.at[k, at], col_r.at[k, 3 - d, at]
        return pltpu.make_async_remote_copy(
            src_ref=src,
            dst_ref=dst,
            send_sem=ha_send.at[k, part, d],
            recv_sem=ha_recv.at[k, part, d ^ 1],
            device_id=targets[d],
            device_id_type=MESH,
        )

    def gather(k, peer):
        return pltpu.make_async_remote_copy(
            src_ref=all_r.at[k, me],
            dst_ref=all_r.at[k, me],
            send_sem=ga_send.at[k],
            recv_sem=ga_recv.at[k],
            device_id=peer,
            device_id_type=MESH,
        )

    def gathered(k, sem):
        others = all_r.at[k, pl.ds(1, ndev - 1)]
        pltpu.make_async_copy(others, others, sem.at[k]).wait()

    def on_faces(act):
        for d in range(4):

            @pl.when(conds[d])
            def _():
                act(d)

    loads[0].wait()
    loads[1].wait()

    @pl.loop(0, ct // GROUP)
    def _(group):
        packed = zero
        for u in range(GROUP):
            t = group * GROUP + u
            value = lookup(ids_ref[t], stiff_ref)
            stiff[t + 1] = value
            srow_s[0, pl.ds(t, 1), :] = value[0:1]
            srow_s[1, pl.ds(t, 1), :] = value[rows - 1 : rows]
            packed = pack(value, u, packed)
        scol_s[group] = packed

    stiff[0] = stiff[ct]
    stiff[ct + 1] = stiff[1]

    pl.semaphore_wait(barrier, ndev - 1)
    on_faces(lambda d: stiff_copy(d).start())

    e_row, e_col = grid_of(lanes, lanes)
    fold = jnp.where(e_row // AA == e_col % band_c, 1.0, 0.0)
    k_row, k_col = grid_of(4 * rows, lanes)
    keep = k_row // AR == (j + rows - k_col // band_c) % rows

    def restrict_and_send(k, sums):
        folded = dot(jnp.concatenate(sums, axis=0), fold)
        all_r[k, me] = jnp.sum(jnp.where(keep, folded, 0.0), axis=0, keepdims=True)
        each_peer(lambda peer: gather(k, peer).start())

    loads[2].wait()

    def sum_pass(chunk, sums):
        sums = list(sums)
        for u in range(CHUNK):
            for c in range(4):
                sums[c] = sums[c] + rhs_ref[c // 2, c % 2, chunk * CHUNK + u]
        return tuple(sums)

    restrict_and_send(0, lax.fori_loop(0, chunks, sum_pass, (zero,) * 4))
    for load_in in loads[3:]:
        load_in.wait()

    ax_row, ax_col = grid_of(lanes, ga)
    own = jnp.where(ax_row // AA + j * band_c == ax_col, 1.0, 0.0)
    half = lanes // 2
    side = jnp.where(ax_row % 2 == 0, j * band_c - 1, (j + 1) * band_c) == ax_col
    edges = [jnp.where(side & (ax_row // half == p), 1.0, 0.0) for p in range(2)]
    for h in range(2):
        if ga < lanes:
            axmat[h] = jnp.zeros(axmat.shape[1:], jnp.float32)
        axmat[h, 0:lanes, 0:ga] = dot(own, axial_ref[0, h])
        axmat[h, lanes : 2 * lanes, 0:ga] = dot(own, axial_ref[1, h])
        axmat[h, 2 * lanes : 3 * lanes, 0:ga] = dot(edges[0], axial_ref[0, h]) + dot(
            edges[1], axial_ref[1, h]
        )

    per = 2 * rows
    cdev = 4 * band_r
    r_row, r_col = grid_of(4 * per, gr)
    r_row = r_row % per
    want = jnp.where(
        r_row < rows,
        r_row // AR + i * band_r,
        jnp.where(
            r_row == rows, i * band_r - 1, jnp.where(r_row == rows + 1, (i + 1) * band_r, -1)
        ),
    )
    r_sel = jnp.where(want == r_col, 1.0, 0.0)
    c_row, c_col = grid_of(gr, nrad * cdev)
    c_sel = jnp.where((c_col // cdev) * band_r + c_col % band_r == c_row, 1.0, 0.0)
    m_row, m_col = grid_of(4 * per, nrad * cdev)
    m_out = m_row // per
    m_in = (m_col % cdev) // band_r
    first = jnp.zeros((4 * per, nrad * cdev), jnp.float32)
    second = first
    for h in range(2):
        same = (m_out == m_in) & (m_out % 2 == h)
        to_re = (m_out == h) & (m_in == 2 + h)
        to_im = (m_out == 2 + h) & (m_in == h)
        real = dot(dot(r_sel, radial_ref[0, h]), c_sel)
        imag = dot(dot(r_sel, radial_ref[1, h]), c_sel)
        first = jnp.where(same, real, first)
        first = jnp.where(to_re, -imag, first)
        first = jnp.where(to_im, imag, first)
        second = jnp.where(same, -imag, second)
        second = jnp.where(to_re, -real, second)
        second = jnp.where(to_im, real, second)
    radmat[:, 0 : nrad * cdev] = first
    radmat[:, nrad * cdev : 2 * nrad * cdev] = second

    p_row, _ = grid_of(nrad * cdev, 3 * lanes)
    odd_harm = (p_row // band_r) % 2 == 1

    def finish_coarse(k):
        gathered(k, ga_recv)

        tiles = []
        for a in range(nrad):
            tile = zero
            for b in range(nax):
                tile = jnp.where((lane // band_c + row) % rows == b, all_r[k, a * nax + b], tile)
            tile = pltpu.roll(tile, 0, 1, stride=band_c, stride_axis=0)
            tiles.append(tile)
        whole = jnp.concatenate(tiles, axis=0)
        prod = [
            lax.dot_general(
                whole,
                axmat[h],
                (((1,), (1,)), ((), ())),
                precision=HIGHEST,
                preferred_element_type=jnp.float32,
            )
            for h in range(2)
        ]
        prod = jnp.where(odd_harm, prod[1], prod[0])
        a = prod[:, 0:lanes]
        b = prod[:, lanes : 2 * lanes]
        e = prod[:, 2 * lanes : 3 * lanes]
        f = pltpu.roll(e, half, 1)
        mixed = jnp.concatenate(
            [jnp.concatenate([a, e], axis=1), jnp.concatenate([b, f], axis=1)], axis=0
        )
        return dot(radmat[...], mixed)

    on_faces(lambda d: stiff_copy(d ^ 1).wait_recv())

    mass = [mass_ref[0], mass_ref[1]]

    def smooth(t, rr, ri, h):
        d_re, d_im, scale = dr[h, t], di[t], sc[h, t]
        return (d_re * rr + d_im * ri) * scale, (d_re * ri - d_im * rr) * scale

    per_group = GROUP // CHUNK
    for n in range(ct // GROUP):
        merged = jnp.where(odd_lane, scol_r[1, n], scol_r[0, n])
        for m in range(per_group):
            scol_m[n * per_group + m] = (
                merged if m == 0 else pltpu.roll(merged, lanes - 2 * CHUNK * m, 1)
            )

    def setup_step(t, u, packed, faces, beside, moved):
        value = stiff[t + 1]
        up, dn, lo, hi = around(
            value,
            srow_r[0, pl.ds(t, 1), :],
            srow_r[1, pl.ds(t, 1), :],
            pltpu.roll(beside, lanes - 1 - 2 * u, 1),
        )
        c_up, c_dn = 0.5 * (value + up), 0.5 * (value + dn)
        c_lo, c_hi = 0.5 * (value + lo), 0.5 * (value + hi)
        c_be, c_ah = 0.5 * (value + stiff[t]), 0.5 * (value + stiff[t + 2])
        wr_up[t] = c_up
        wr_dn[t] = c_dn
        wa_lo[t] = c_lo
        wa_hi[t] = c_hi
        w_rows[0, pl.ds(t, 1), :] = c_up[0:1]
        w_rows[1, pl.ds(t, 1), :] = c_dn[rows - 1 : rows]
        wt[t] = c_be
        wt[t + 1] = c_ah
        total = c_dn + c_up + c_hi + c_lo + c_ah + c_be
        density = lookup(ids_ref[t], dens_ref)
        dens[t] = density
        moved = [m + w for m, w in zip(moved, (c_up, c_dn, c_lo, c_hi, density))]
        d_im = LOSS_FACTOR * total
        di[t] = d_im
        y = [None] * 4
        for h in range(2):
            d_re = total - mass[h] * density
            scale = RELAXATION / (d_re * d_re + d_im * d_im)
            dr[h, t] = d_re
            sc[h, t] = scale
            rr, ri = rhs_ref[0, h, t], rhs_ref[1, h, t]
            y[h] = (d_re * rr + d_im * ri) * scale
            y[2 + h] = (d_re * ri - d_im * rr) * scale
            sol_ref[0, h, t] = y[h]
            sol_ref[1, h, t] = y[2 + h]
        for c in range(4):
            packed = pack(y[c], c * CHUNK + u, packed)
        faces = pack(jnp.where(lane == 0, c_lo, c_hi), u, faces)
        return packed, faces, moved

    def in_parts(k, step, carry):
        def one_part(part, carry):
            carry = lax.fori_loop(
                0,
                part_chunks,
                lambda n, carry: step(part * part_chunks + n, carry),
                carry,
                unroll=True,
            )
            on_faces(lambda d: halo_copy(k, part, d).start())
            return carry

        return lax.fori_loop(0, PARTS, one_part, carry)

    def setup_chunk(chunk, moved):
        packed = zero
        faces = zero
        beside = scol_m[chunk]
        for u in range(CHUNK):
            packed, faces, moved = setup_step(chunk * CHUNK + u, u, packed, faces, beside, moved)
        col_s[0, chunk] = packed
        faces = faces + pltpu.roll(faces, 2 * CHUNK, 1)
        w_cols[chunk] = faces + pltpu.roll(faces, 4 * CHUNK, 1)
        return tuple(moved)

    moved = in_parts(0, setup_chunk, (zero,) * 5)

    trig = [[], []]
    for h in range(2):
        angle = jnp.full((rows, lanes), harm_ref[h], jnp.int32).astype(jnp.float32) * (
            2.0 * jnp.pi / NSECT
        )
        trig[0].append(jnp.cos(angle))
        trig[1].append(jnp.sin(angle))
    trig = trig[0] + trig[1]

    def load(t):
        return [sol_ref[c // 2, c % 2, t] for c in range(4)]

    def apply_operator(k):
        start = load(0)
        beyond = turn(trig, start, 1.0)
        before = turn(trig, load(ct - 1), -1.0)

        def chunk_pass(chunk, carry):
            xm, x, sums = list(carry[0:4]), list(carry[4:8]), list(carry[8:])
            for u in range(CHUNK):
                t = chunk * CHUNK + u
                if u < CHUNK - 1:
                    xp = load(t + 1)
                else:
                    ended = t == ct - 1
                    xp = load(jnp.minimum(t + 1, ct - 1))
                    xp = [jnp.where(ended, beyond[c], xp[c]) for c in range(4)]
                c_up, c_dn, c_lo, c_hi = wr_up[t], wr_dn[t], wa_lo[t], wa_hi[t]
                c_be, c_ah = wt[t], wt[t + 1]
                nb = []
                for c in range(4):
                    up = jnp.where(row == 0, 0.0, pltpu.roll(x[c], 1, 0))
                    dn = jnp.where(row == rows - 1, 0.0, pltpu.roll(x[c], rows - 1, 0))
                    lo = jnp.where(lane == 0, 0.0, pltpu.roll(x[c], 1, 1))
                    hi = jnp.where(lane == lanes - 1, 0.0, pltpu.roll(x[c], lanes - 1, 1))
                    nb.append(
                        (c_dn * dn + c_up * up)
                        + (c_hi * hi + c_lo * lo)
                        + (c_ah * xp[c] + c_be * xm[c])
                    )
                nb = lossy(nb)
                d_im = di[t]
                for h in range(2):
                    d_re = dr[h, t]
                    re, im = h, 2 + h
                    val_re = rhs_ref[0, h, t] - (d_re * x[re] - d_im * x[im] - nb[re])
                    val_im = rhs_ref[1, h, t] - (d_re * x[im] + d_im * x[re] - nb[im])
                    val_ref[0, h, t] = val_re
                    val_ref[1, h, t] = val_im
                    sums[re] = sums[re] + val_re
                    sums[im] = sums[im] + val_im
                xm, x = x, xp
            return tuple(xm) + tuple(x) + tuple(sums)

        carry = tuple(before) + tuple(start) + (zero,) * 4
        return lax.fori_loop(0, chunks, chunk_pass, carry, unroll=4)[8:]

    def fix_faces(k, sums):
        @pl.loop(0, PARTS)
        def _(part):
            on_faces(lambda d: halo_copy(k, part, d ^ 1).wait_recv())

        def chunk_fix(chunk, carry):
            out = []
            at = pl.ds(pl.multiple_of(chunk * CHUNK, CHUNK), CHUNK)
            for side in range(2):
                weight = w_rows[side, at]
                term = lossy([weight * row_r[k, side, c // 2, c % 2, at] for c in range(4)])
                for c in range(4):
                    fix_rows[side, c, at] = term[c]
                    out.append(carry[4 * side + c] + term[c])
            term = w_cols[chunk] * jnp.where(
                odd_lane,
                pltpu.roll(col_r[k, 0, chunk], 1, 1),
                pltpu.roll(col_r[k, 1, chunk], lanes - 1, 1),
            )
            turned = jnp.where(
                pair < 2 * CHUNK,
                -pltpu.roll(term, lanes - 4 * CHUNK, 1),
                pltpu.roll(term, 4 * CHUNK, 1),
            )
            term = term + LOSS_FACTOR * turned
            fix_cols[chunk] = term
            return tuple(out) + (carry[8] + term,)

        carry = lax.fori_loop(0, chunks, chunk_fix, (zero,) * 9, unroll=4)
        beside = carry[8]
        step = 1
        while step < CHUNK:
            beside = beside + pltpu.roll(beside, lanes - 2 * step, 1)
            step *= 2
        outs = []
        for c in range(4):
            edge = pltpu.roll(beside, lanes - 1 - 2 * c * CHUNK, 1)
            outs.append(
                sums[c]
                + jnp.where(row == 0, jnp.sum(carry[c], axis=0, keepdims=True), 0.0)
                + jnp.where(row == rows - 1, jnp.sum(carry[4 + c], axis=0, keepdims=True), 0.0)
                + jnp.where((lane == 0) | (lane == lanes - 1), edge, 0.0)
            )
        return outs

    for k in range(ITERS):
        final = k == ITERS - 1
        sums = apply_operator(k)
        coarse = finish_coarse(k)
        corr = [coarse[c * per : c * per + rows, 0:lanes] for c in range(4)]
        apart = [[], [], [], []]
        for c in range(4):
            line = c * per + rows
            beside = coarse[c * per : c * per + rows, lanes : 2 * lanes]
            shifted = (
                jnp.where(row == 0, coarse[line : line + 1, 0:lanes], pltpu.roll(corr[c], 1, 0)),
                jnp.where(
                    row == rows - 1,
                    coarse[line + 1 : line + 2, 0:lanes],
                    pltpu.roll(corr[c], rows - 1, 0),
                ),
                jnp.where(lane == 0, beside, pltpu.roll(corr[c], 1, 1)),
                jnp.where(
                    lane == lanes - 1,
                    pltpu.roll(beside, lanes - 2, 1),
                    pltpu.roll(corr[c], lanes - 1, 1),
                ),
            )
            for n in range(4):
                apart[n].append(corr[c] - shifted[n])
        push = [lossy(apart[n]) for n in range(4)]
        push.append([mass[c % 2] * corr[c] for c in range(4)])
        ends = []
        for sign, weight in ((-1.0, wt[0]), (1.0, wt[ct])):
            over = turn(trig, corr, sign)
            ends.append([weight * x for x in lossy([corr[c] - over[c] for c in range(4)])])
        sums = fix_faces(k, sums)
        if not final:
            restrict_and_send(
                k + 1,
                [
                    sums[c] - coarse_change(moved, push, c) - ends[0][c] - ends[1][c]
                    for c in range(4)
                ],
            )
        for c in range(4):
            val_ref[c // 2, c % 2, 0] = val_ref[c // 2, c % 2, 0] - ends[0][c]
            val_ref[c // 2, c % 2, ct - 1] = val_ref[c // 2, c % 2, ct - 1] - ends[1][c]
        if final:
            for c in range(4):
                corr_ref[c] = corr[c]
                for n in range(5):
                    push_ref[n, c] = push[n][c]
            break

        @pl.loop(0, PARTS)
        def _(part):
            on_faces(lambda d: halo_copy(k, part, d).wait_send())

        def update_chunk(chunk, nothing):
            packed = zero
            for u in range(CHUNK):
                t = chunk * CHUNK + u
                weights = (wr_up[t], wr_dn[t], wa_lo[t], wa_hi[t], dens[t])
                res = [
                    (val_ref[c // 2, c % 2, t] - coarse_change(weights, push, c))
                    + face_terms(fix_rows, fix_cols, t, chunk, c, u)
                    for c in range(4)
                ]
                x = load(t)
                y = [None] * 4
                for h in range(2):
                    a, b = smooth(t, res[h], res[2 + h], h)
                    y[h], y[2 + h] = (x[h] + corr[h]) + a, (x[2 + h] + corr[2 + h]) + b
                for c in range(4):
                    sol_ref[c // 2, c % 2, t] = y[c]
                    packed = pack(y[c], c * CHUNK + u, packed)
            col_s[k + 1, chunk] = packed
            return nothing

        in_parts(k + 1, update_chunk, 0)

    on_faces(lambda d: stiff_copy(d).wait_send())

    @pl.loop(0, PARTS)
    def _(part):
        on_faces(lambda d: halo_copy(ITERS - 1, part, d).wait_send())

    for k in range(ITERS):
        gathered(k, ga_send)


def last_pass(
    sol_ref,
    val_ref,
    wr_up,
    wr_dn,
    wa_lo,
    wa_hi,
    dens,
    corr_ref,
    push_ref,
    fix_rows,
    fix_cols,
    sol_hbm,
    res_hbm,
    sol_out,
    res_out,
    sem,
):
    ct = sol_ref.shape[2]
    chunks = ct // CHUNK
    corr = [corr_ref[c] for c in range(4)]
    push = [[push_ref[n, c] for c in range(4)] for n in range(5)]

    def put(n, chunk):
        src, dst = ((sol_out, sol_hbm), (res_out, res_hbm))[n]
        at = pl.ds(chunk * CHUNK, CHUNK)
        return pltpu.make_async_copy(src.at[:, :, at], dst.at[:, :, at], sem.at[n, chunk])

    @pl.loop(0, chunks)
    def _(chunk):
        for u in range(CHUNK):
            t = chunk * CHUNK + u
            weights = (wr_up[t], wr_dn[t], wa_lo[t], wa_hi[t], dens[t])
            for c in range(4):
                sol_out[c // 2, c % 2, t] = sol_ref[c // 2, c % 2, t] + corr[c]
                res_out[c // 2, c % 2, t] = (
                    val_ref[c // 2, c % 2, t] - coarse_change(weights, push, c)
                ) + face_terms(fix_rows, fix_cols, t, chunk, c, u)
        for n in range(2):
            put(n, chunk).start()

    @pl.loop(0, chunks)
    def _(chunk):
        for n in range(2):
            put(n, chunk).wait()


def local(rhs, mat_ids, stiff_table, dens_table, mass_shift, harmonic, radial_factor, axial_factor):
    nrad = lax.axis_size("radial")
    nax = lax.axis_size("axial")
    ct, rows, lanes = mat_ids.shape
    vmem = pl.BlockSpec(memory_space=pltpu.VMEM)
    hbm = pl.BlockSpec(memory_space=pltpu.HBM)
    f32 = jnp.float32
    field = (ct, rows, lanes)
    chunks = ct // CHUNK
    groups = ct // GROUP
    cdev = 4 * (rows // AR)
    ndev = nrad * nax
    dma = pltpu.SemaphoreType.DMA
    inputs = (
        rhs,
        mat_ids,
        stiff_table,
        dens_table,
        mass_shift,
        harmonic,
        radial_factor,
        axial_factor,
    )
    held = (
        rhs.shape,
        rhs.shape,
        field,
        field,
        field,
        field,
        field,
        (4, rows, lanes),
        (5, 4, rows, lanes),
        (2, 4, ct, lanes),
        (chunks, rows, lanes),
    )
    state = pl.pallas_call(
        functools.partial(kernel, nrad, nax),
        out_shape=tuple(pltpu.VMEM(shape, f32) for shape in held),
        in_specs=[hbm] * 8,
        out_specs=(vmem,) * len(held),
        scratch_shapes=[
            pltpu.VMEM(rhs.shape, f32),
            pltpu.VMEM(field, jnp.int32),
            pltpu.SMEM(stiff_table.shape, f32),
            pltpu.SMEM(dens_table.shape, f32),
            pltpu.SMEM(mass_shift.shape, f32),
            pltpu.SMEM(harmonic.shape, jnp.int32),
            pltpu.VMEM(radial_factor.shape, f32),
            pltpu.VMEM(axial_factor.shape, f32),
            dma((8,)),
            pltpu.VMEM((ct + 2, rows, lanes), f32),
            pltpu.VMEM((ct + 1, rows, lanes), f32),
            pltpu.VMEM((2,) + field, f32),
            pltpu.VMEM(field, f32),
            pltpu.VMEM((2,) + field, f32),
            pltpu.VMEM((2, ct, lanes), f32),
            pltpu.VMEM((chunks, rows, lanes), f32),
            pltpu.VMEM((2, ct, lanes), f32),
            pltpu.VMEM((2, ct, lanes), f32),
            pltpu.VMEM((groups, rows, lanes), f32),
            pltpu.VMEM((2, groups, rows, lanes), f32),
            pltpu.VMEM((chunks, rows, lanes), f32),
            pltpu.VMEM((ITERS, 2, 2, 2, ct, lanes), f32),
            pltpu.VMEM((ITERS, chunks, rows, lanes), f32),
            pltpu.VMEM((ITERS, 2, chunks, rows, lanes), f32),
            pltpu.VMEM((ITERS, ndev, 1, lanes), f32),
            pltpu.VMEM((2, 3 * lanes, lanes), f32),
            pltpu.VMEM((8 * rows, 2 * nrad * cdev), f32),
            dma((4,)),
            dma((4,)),
            dma((ITERS, PARTS, 4)),
            dma((ITERS, PARTS, 4)),
            dma((ITERS,)),
            dma((ITERS,)),
        ],
        compiler_params=pltpu.CompilerParams(
            collective_id=0, has_side_effects=True, vmem_limit_bytes=48 * 1024 * 1024
        ),
    )(*[pltpu.with_memory_space_constraint(x, pltpu.HBM) for x in inputs])
    return pl.pallas_call(
        last_pass,
        out_shape=(jax.ShapeDtypeStruct(rhs.shape, f32), jax.ShapeDtypeStruct(rhs.shape, f32)),
        in_specs=[vmem] * len(held),
        out_specs=(hbm, hbm),
        scratch_shapes=[
            pltpu.VMEM(rhs.shape, f32),
            pltpu.VMEM(rhs.shape, f32),
            dma((2, chunks)),
        ],
        compiler_params=pltpu.CompilerParams(vmem_limit_bytes=32 * 1024 * 1024),
    )(*[pltpu.with_memory_space_constraint(x, pltpu.VMEM) for x in state])


def solution(mesh):
    return jax.shard_map(
        local,
        mesh=mesh,
        in_specs=(
            P(None, None, None, "radial", "axial"),
            P(None, "radial", "axial"),
            P(),
            P(),
            P(),
            P(),
            P(),
            P(),
        ),
        out_specs=(P(None, None, None, "radial", "axial"), P(None, None, None, "radial", "axial")),
        check_vma=False,
    )
```

```python
import functools

import jax
import jax.numpy as jnp
from jax import lax
from jax.experimental import pallas as pl
from jax.experimental.pallas import tpu as pltpu
from jax.sharding import PartitionSpec as P

ITERS = 3
NSECT = 24
AR = 4
AA = 8
LOSS_FACTOR = 0.2
RELAXATION = 0.6
MESH = pl.DeviceIdType.MESH
HIGHEST = lax.Precision.HIGHEST
CHUNK = 8
PARTS = 6
GROUP = 32


def dot(a, b):
    return jnp.dot(a, b, precision=HIGHEST, preferred_element_type=jnp.float32)


def dot16(a, b):
    return jnp.dot(a, b, preferred_element_type=jnp.float32)


def split(x):
    high = x.astype(jnp.bfloat16)
    return high, (x - high.astype(jnp.float32)).astype(jnp.bfloat16)


def left_parts(x):
    high, low = split(x)
    return jnp.concatenate([high, low, high], axis=1)


def right_parts(x, axis):
    high, low = split(x)
    return jnp.concatenate([high, high, low], axis=axis)


def grid_of(rows, lanes):
    return (
        lax.broadcasted_iota(jnp.int32, (rows, lanes), 0),
        lax.broadcasted_iota(jnp.int32, (rows, lanes), 1),
    )


def around(value, up, dn, edge):
    rows, lanes = value.shape
    row, lane = grid_of(rows, lanes)
    return (
        jnp.where(row == 0, up, pltpu.roll(value, 1, 0)),
        jnp.where(row == rows - 1, dn, pltpu.roll(value, rows - 1, 0)),
        pltpu.roll(jnp.where(lane == lanes - 1, edge, value), 1, 1),
        pltpu.roll(jnp.where(lane == 0, edge, value), lanes - 1, 1),
    )


def face_terms(fix_rows, fix_cols, t, chunk, c, u):
    rows, lanes = fix_cols.shape[1:]
    row, lane = grid_of(rows, lanes)
    edge = pltpu.roll(fix_cols[chunk], lanes - 1 - 2 * (c * CHUNK + u), 1)
    along = jnp.where(
        row == 0,
        fix_rows[0, c, pl.ds(t, 1), :],
        jnp.where(row == rows - 1, fix_rows[1, c, pl.ds(t, 1), :], 0.0),
    )
    return along + jnp.where((lane == 0) | (lane == lanes - 1), edge, 0.0)


def lossy(x):
    return [x[h] - LOSS_FACTOR * x[2 + h] for h in range(2)] + [
        x[2 + h] + LOSS_FACTOR * x[h] for h in range(2)
    ]


def coarse_change(weights, push, c):
    w_up, w_dn, w_lo, w_hi, dens = weights
    return ((w_up * push[0][c] + w_dn * push[1][c]) + (w_lo * push[2][c] + w_hi * push[3][c])) - (
        dens * push[4][c]
    )


def turn(trig, x, sign):
    cosines, sines = trig[0:2], trig[2:4]
    return [cosines[h] * x[h] - sign * sines[h] * x[2 + h] for h in range(2)] + [
        sign * sines[h] * x[h] + cosines[h] * x[2 + h] for h in range(2)
    ]


def kernel(
    nrad,
    nax,
    rhs_hbm,
    ids_hbm,
    stiff_hbm,
    dens_hbm,
    mass_hbm,
    harm_hbm,
    radial_hbm,
    axial_hbm,
    sol_ref,
    val_ref,
    wr_up,
    wr_dn,
    wa_lo,
    wa_hi,
    dens,
    corr_ref,
    push_ref,
    fix_rows,
    fix_cols,
    rhs_ref,
    ids_ref,
    stiff_ref,
    dens_ref,
    mass_ref,
    harm_ref,
    radial_ref,
    axial_ref,
    in_sem,
    stiff,
    wt,
    dr,
    di,
    sc,
    w_rows,
    w_cols,
    srow_s,
    srow_r,
    scol_s,
    scol_r,
    scol_m,
    row_r,
    col_s,
    col_r,
    all_r,
    axmat,
    radmat,
    st_send,
    st_recv,
    ha_send,
    ha_recv,
    ga_send,
    ga_recv,
):
    loads = [
        pltpu.make_async_copy(src, dst, in_sem.at[n])
        for n, (src, dst) in enumerate(
            (
                (stiff_hbm, stiff_ref),
                (ids_hbm, ids_ref),
                (rhs_hbm, rhs_ref),
                (dens_hbm, dens_ref),
                (mass_hbm, mass_ref),
                (harm_hbm, harm_ref),
                (radial_hbm, radial_ref),
                (axial_hbm, axial_ref),
            )
        )
    ]
    for load_in in loads:
        load_in.start()
    ct = rhs_ref.shape[2]
    rows, lanes = rhs_ref.shape[3:]
    gr = radial_ref.shape[2]
    ga = axial_ref.shape[2]
    band_r = rows // AR
    band_c = lanes // AA
    chunks = ct // CHUNK
    ndev = nrad * nax
    i = lax.axis_index("radial")
    j = lax.axis_index("axial")
    me = i * nax + j
    has_up, has_dn = i > 0, i < nrad - 1
    has_lo, has_hi = j > 0, j < nax - 1
    conds = (has_up, has_dn, has_lo, has_hi)
    targets = ({"radial": i - 1}, {"radial": i + 1}, {"axial": j - 1}, {"axial": j + 1})

    def each_peer(act):
        def along(a):
            to = i + a
            to = jnp.where(to >= nrad, to - nrad, to)
            for b in range(nax):
                at = j + b
                act({"radial": to, "axial": jnp.where(at >= nax, at - nax, at)})

        for b in range(1, nax):
            at = j + b
            act({"radial": i, "axial": jnp.where(at >= nax, at - nax, at)})
        if nrad <= 8:
            for a in range(1, nrad):
                along(a)
        else:
            pl.loop(1, nrad)(along)

    barrier = pltpu.get_barrier_semaphore()
    each_peer(
        lambda peer: pl.semaphore_signal(barrier, inc=1, device_id=peer, device_id_type=MESH)
    )

    for d in range(4):

        @pl.when(jnp.logical_not(conds[d]))
        def _():
            if d < 2:
                srow_r[d] = jnp.zeros(srow_r.shape[1:], jnp.float32)
                for k in range(ITERS):
                    row_r[k, d] = jnp.zeros(row_r.shape[2:], jnp.float32)
            else:
                scol_r[d - 2] = jnp.zeros(scol_r.shape[1:], jnp.float32)
                for k in range(ITERS):
                    col_r[k, d - 2] = jnp.zeros(col_r.shape[2:], jnp.float32)

    row, lane = grid_of(rows, lanes)
    zero = jnp.zeros((rows, lanes), jnp.float32)
    pair = lane // 2
    odd_lane = lane % 2 == 1

    def lookup(ids, table):
        value = jnp.full(ids.shape, table[0], jnp.float32)
        for entry in range(1, table.shape[0]):
            value = jnp.where(ids == entry, table[entry], value)
        return value

    def pack(value, at, packed):
        return jnp.where(pair == at, pltpu.roll(value, (2 * at + 1) % lanes, 1), packed)

    def stiff_copy(d):
        if d < 2:
            src, dst = srow_s.at[d], srow_r.at[1 - d]
        else:
            src, dst = scol_s, scol_r.at[3 - d]
        return pltpu.make_async_remote_copy(
            src_ref=src,
            dst_ref=dst,
            send_sem=st_send.at[d],
            recv_sem=st_recv.at[d ^ 1],
            device_id=targets[d],
            device_id_type=MESH,
        )

    part_chunks = chunks // PARTS
    part_ct = ct // PARTS

    def halo_copy(k, part, d):
        if d < 2:
            at = pl.ds(part * part_ct, part_ct)
            line = 0 if d == 0 else rows - 1
            src, dst = sol_ref.at[:, :, at, line], row_r.at[k, 1 - d, :, :, at]
        else:
            at = pl.ds(part * part_chunks, part_chunks)
            src, dst = col_s.at[k, at], col_r.at[k, 3 - d, at]
        return pltpu.make_async_remote_copy(
            src_ref=src,
            dst_ref=dst,
            send_sem=ha_send.at[k, d],
            recv_sem=ha_recv.at[k, d ^ 1],
            device_id=targets[d],
            device_id_type=MESH,
        )

    def halo_done(k, d, sem):
        got = row_r.at[k, d] if d < 2 else col_r.at[k, d - 2]
        pltpu.make_async_copy(got, got, sem.at[k, d]).wait()

    def gather(k, peer):
        return pltpu.make_async_remote_copy(
            src_ref=all_r.at[k, me],
            dst_ref=all_r.at[k, me],
            send_sem=ga_send.at[k],
            recv_sem=ga_recv.at[k],
            device_id=peer,
            device_id_type=MESH,
        )

    def gathered(k, sem):
        others = all_r.at[k, pl.ds(1, ndev - 1)]
        pltpu.make_async_copy(others, others, sem.at[k]).wait()

    def on_faces(act):
        for d in range(4):

            @pl.when(conds[d])
            def _():
                act(d)

    loads[0].wait()
    loads[1].wait()

    @pl.loop(0, ct // GROUP)
    def _(group):
        packed = zero
        for u in range(GROUP):
            t = group * GROUP + u
            value = lookup(ids_ref[t], stiff_ref)
            stiff[t + 1] = value
            srow_s[0, pl.ds(t, 1), :] = value[0:1]
            srow_s[1, pl.ds(t, 1), :] = value[rows - 1 : rows]
            packed = pack(value, u, packed)
        scol_s[group] = packed

    stiff[0] = stiff[ct]
    stiff[ct + 1] = stiff[1]

    pl.semaphore_wait(barrier, ndev - 1)
    on_faces(lambda d: stiff_copy(d).start())

    e_row, e_col = grid_of(lanes, lanes)
    fold = jnp.where(e_row // AA == e_col % band_c, 1.0, 0.0).astype(jnp.bfloat16)
    fold = jnp.concatenate([fold, fold], axis=0)
    k_row, k_col = grid_of(4 * rows, lanes)
    keep = k_row // AR == (j + rows - k_col // band_c) % rows

    def restrict_and_send(k, sums):
        folded = dot16(jnp.concatenate(split(jnp.concatenate(sums, axis=0)), axis=1), fold)
        all_r[k, me] = jnp.sum(jnp.where(keep, folded, 0.0), axis=0, keepdims=True)
        each_peer(lambda peer: gather(k, peer).start())

    loads[2].wait()

    def sum_pass(chunk, sums):
        sums = list(sums)
        for u in range(CHUNK):
            for c in range(4):
                sums[c] = sums[c] + rhs_ref[c // 2, c % 2, chunk * CHUNK + u]
        return tuple(sums)

    restrict_and_send(0, lax.fori_loop(0, chunks, sum_pass, (zero,) * 4))
    for load_in in loads[3:]:
        load_in.wait()

    ax_row, ax_col = grid_of(lanes, ga)
    own = jnp.where(ax_row // AA + j * band_c == ax_col, 1.0, 0.0)
    half = lanes // 2
    side = jnp.where(ax_row % 2 == 0, j * band_c - 1, (j + 1) * band_c) == ax_col
    edges = [jnp.where(side & (ax_row // half == p), 1.0, 0.0) for p in range(2)]
    spare = [jnp.zeros((3 * lanes, lanes - ga), jnp.float32)] if ga < lanes else []
    for h in range(2):
        wide = jnp.concatenate(
            [
                dot(own, axial_ref[0, h]),
                dot(own, axial_ref[1, h]),
                dot(edges[0], axial_ref[0, h]) + dot(edges[1], axial_ref[1, h]),
            ],
            axis=0,
        )
        axmat[h] = right_parts(jnp.concatenate([wide] + spare, axis=1), 1)

    per = 2 * rows
    cdev = 4 * band_r
    r_row, r_col = grid_of(4 * per, gr)
    r_row = r_row % per
    want = jnp.where(
        r_row < rows,
        r_row // AR + i * band_r,
        jnp.where(
            r_row == rows, i * band_r - 1, jnp.where(r_row == rows + 1, (i + 1) * band_r, -1)
        ),
    )
    r_sel = jnp.where(want == r_col, 1.0, 0.0)
    c_row, c_col = grid_of(gr, nrad * cdev)
    c_sel = jnp.where((c_col // cdev) * band_r + c_col % band_r == c_row, 1.0, 0.0)
    m_row, m_col = grid_of(4 * per, nrad * cdev)
    m_out = m_row // per
    m_in = (m_col % cdev) // band_r
    first = jnp.zeros((4 * per, nrad * cdev), jnp.float32)
    second = first
    for h in range(2):
        same = (m_out == m_in) & (m_out % 2 == h)
        to_re = (m_out == h) & (m_in == 2 + h)
        to_im = (m_out == 2 + h) & (m_in == h)
        real = dot(dot(r_sel, radial_ref[0, h]), c_sel)
        imag = dot(dot(r_sel, radial_ref[1, h]), c_sel)
        first = jnp.where(same, real, first)
        first = jnp.where(to_re, -imag, first)
        first = jnp.where(to_im, imag, first)
        second = jnp.where(same, -imag, second)
        second = jnp.where(to_re, -real, second)
        second = jnp.where(to_im, real, second)
    radmat[...] = left_parts(jnp.concatenate([first, second], axis=1))

    p_row, _ = grid_of(nrad * cdev, 3 * lanes)
    odd_harm = (p_row // band_r) % 2 == 1

    def finish_coarse(k):
        gathered(k, ga_recv)

        tiles = []
        for a in range(nrad):
            tile = zero
            for b in range(nax):
                tile = jnp.where((lane // band_c + row) % rows == b, all_r[k, a * nax + b], tile)
            tile = pltpu.roll(tile, 0, 1, stride=band_c, stride_axis=0)
            tiles.append(tile)
        whole = left_parts(jnp.concatenate(tiles, axis=0))
        prod = [
            lax.dot_general(
                whole,
                axmat[h],
                (((1,), (1,)), ((), ())),
                preferred_element_type=jnp.float32,
            )
            for h in range(2)
        ]
        prod = jnp.where(odd_harm, prod[1], prod[0])
        a = prod[:, 0:lanes]
        b = prod[:, lanes : 2 * lanes]
        e = prod[:, 2 * lanes : 3 * lanes]
        f = pltpu.roll(e, half, 1)
        mixed = jnp.concatenate(
            [jnp.concatenate([a, e], axis=1), jnp.concatenate([b, f], axis=1)], axis=0
        )
        return dot16(radmat[...], right_parts(mixed, 0))

    on_faces(lambda d: stiff_copy(d ^ 1).wait_recv())

    mass = [mass_ref[0], mass_ref[1]]

    def smooth(t, rr, ri, h):
        d_re, d_im, scale = dr[h, t], di[t], sc[h, t]
        return (d_re * rr + d_im * ri) * scale, (d_re * ri - d_im * rr) * scale

    per_group = GROUP // CHUNK
    for n in range(ct // GROUP):
        merged = jnp.where(odd_lane, scol_r[1, n], scol_r[0, n])
        for m in range(per_group):
            scol_m[n * per_group + m] = (
                merged if m == 0 else pltpu.roll(merged, lanes - 2 * CHUNK * m, 1)
            )

    def setup_step(t, u, packed, faces, beside, moved):
        value = stiff[t + 1]
        up, dn, lo, hi = around(
            value,
            srow_r[0, pl.ds(t, 1), :],
            srow_r[1, pl.ds(t, 1), :],
            pltpu.roll(beside, lanes - 1 - 2 * u, 1),
        )
        c_up, c_dn = 0.5 * (value + up), 0.5 * (value + dn)
        c_lo, c_hi = 0.5 * (value + lo), 0.5 * (value + hi)
        c_be, c_ah = 0.5 * (value + stiff[t]), 0.5 * (value + stiff[t + 2])
        wr_up[t] = c_up
        wr_dn[t] = c_dn
        wa_lo[t] = c_lo
        wa_hi[t] = c_hi
        w_rows[0, pl.ds(t, 1), :] = c_up[0:1]
        w_rows[1, pl.ds(t, 1), :] = c_dn[rows - 1 : rows]
        wt[t] = c_be
        wt[t + 1] = c_ah
        total = c_dn + c_up + c_hi + c_lo + c_ah + c_be
        density = lookup(ids_ref[t], dens_ref)
        dens[t] = density
        moved = [m + w for m, w in zip(moved, (c_up, c_dn, c_lo, c_hi, density))]
        d_im = LOSS_FACTOR * total
        di[t] = d_im
        y = [None] * 4
        for h in range(2):
            d_re = total - mass[h] * density
            scale = RELAXATION / (d_re * d_re + d_im * d_im)
            dr[h, t] = d_re
            sc[h, t] = scale
            rr, ri = rhs_ref[0, h, t], rhs_ref[1, h, t]
            y[h] = (d_re * rr + d_im * ri) * scale
            y[2 + h] = (d_re * ri - d_im * rr) * scale
            sol_ref[0, h, t] = y[h]
            sol_ref[1, h, t] = y[2 + h]
        for c in range(4):
            packed = pack(y[c], c * CHUNK + u, packed)
        faces = pack(jnp.where(lane == 0, c_lo, c_hi), u, faces)
        return packed, faces, moved

    def in_parts(k, step, carry):
        def one_part(part, carry):
            carry = lax.fori_loop(
                0,
                part_chunks,
                lambda n, carry: step(part * part_chunks + n, carry),
                carry,
                unroll=True,
            )
            on_faces(lambda d: halo_copy(k, part, d).start())
            return carry

        return lax.fori_loop(0, PARTS, one_part, carry)

    def setup_chunk(chunk, moved):
        packed = zero
        faces = zero
        beside = scol_m[chunk]
        for u in range(CHUNK):
            packed, faces, moved = setup_step(chunk * CHUNK + u, u, packed, faces, beside, moved)
        col_s[0, chunk] = packed
        faces = faces + pltpu.roll(faces, 2 * CHUNK, 1)
        w_cols[chunk] = faces + pltpu.roll(faces, 4 * CHUNK, 1)
        return tuple(moved)

    moved = in_parts(0, setup_chunk, (zero,) * 5)

    trig = [[], []]
    for h in range(2):
        angle = jnp.full((rows, lanes), harm_ref[h], jnp.int32).astype(jnp.float32) * (
            2.0 * jnp.pi / NSECT
        )
        trig[0].append(jnp.cos(angle))
        trig[1].append(jnp.sin(angle))
    trig = trig[0] + trig[1]

    def load(t):
        return [sol_ref[c // 2, c % 2, t] for c in range(4)]

    def apply_operator(k):
        start = load(0)
        beyond = turn(trig, start, 1.0)
        before = turn(trig, load(ct - 1), -1.0)

        def chunk_pass(chunk, carry):
            xm, x, sums = list(carry[0:4]), list(carry[4:8]), list(carry[8:])
            for u in range(CHUNK):
                t = chunk * CHUNK + u
                if u < CHUNK - 1:
                    xp = load(t + 1)
                else:
                    ended = t == ct - 1
                    xp = load(jnp.minimum(t + 1, ct - 1))
                    xp = [jnp.where(ended, beyond[c], xp[c]) for c in range(4)]
                c_up, c_dn, c_lo, c_hi = wr_up[t], wr_dn[t], wa_lo[t], wa_hi[t]
                c_be, c_ah = wt[t], wt[t + 1]
                nb = []
                for c in range(4):
                    up = jnp.where(row == 0, 0.0, pltpu.roll(x[c], 1, 0))
                    dn = jnp.where(row == rows - 1, 0.0, pltpu.roll(x[c], rows - 1, 0))
                    lo = jnp.where(lane == 0, 0.0, pltpu.roll(x[c], 1, 1))
                    hi = jnp.where(lane == lanes - 1, 0.0, pltpu.roll(x[c], lanes - 1, 1))
                    nb.append(
                        (c_dn * dn + c_up * up)
                        + (c_hi * hi + c_lo * lo)
                        + (c_ah * xp[c] + c_be * xm[c])
                    )
                nb = lossy(nb)
                d_im = di[t]
                for h in range(2):
                    d_re = dr[h, t]
                    re, im = h, 2 + h
                    val_re = rhs_ref[0, h, t] - (d_re * x[re] - d_im * x[im] - nb[re])
                    val_im = rhs_ref[1, h, t] - (d_re * x[im] + d_im * x[re] - nb[im])
                    val_ref[0, h, t] = val_re
                    val_ref[1, h, t] = val_im
                    sums[re] = sums[re] + val_re
                    sums[im] = sums[im] + val_im
                xm, x = x, xp
            return tuple(xm) + tuple(x) + tuple(sums)

        carry = tuple(before) + tuple(start) + (zero,) * 4
        return lax.fori_loop(0, chunks, chunk_pass, carry, unroll=3)[8:]

    def fix_faces(k, sums):
        on_faces(lambda d: halo_done(k, d, ha_recv))

        def chunk_fix(chunk, carry):
            out = []
            at = pl.ds(pl.multiple_of(chunk * CHUNK, CHUNK), CHUNK)
            for side in range(2):
                weight = w_rows[side, at]
                term = lossy([weight * row_r[k, side, c // 2, c % 2, at] for c in range(4)])
                for c in range(4):
                    fix_rows[side, c, at] = term[c]
                    out.append(carry[4 * side + c] + term[c])
            term = w_cols[chunk] * jnp.where(
                odd_lane,
                pltpu.roll(col_r[k, 0, chunk], 1, 1),
                pltpu.roll(col_r[k, 1, chunk], lanes - 1, 1),
            )
            turned = jnp.where(
                pair < 2 * CHUNK,
                -pltpu.roll(term, lanes - 4 * CHUNK, 1),
                pltpu.roll(term, 4 * CHUNK, 1),
            )
            term = term + LOSS_FACTOR * turned
            fix_cols[chunk] = term
            return tuple(out) + (carry[8] + term,)

        carry = lax.fori_loop(0, chunks, chunk_fix, (zero,) * 9, unroll=6)
        beside = carry[8]
        step = 1
        while step < CHUNK:
            beside = beside + pltpu.roll(beside, lanes - 2 * step, 1)
            step *= 2
        outs = []
        for c in range(4):
            edge = pltpu.roll(beside, lanes - 1 - 2 * c * CHUNK, 1)
            outs.append(
                sums[c]
                + jnp.where(row == 0, jnp.sum(carry[c], axis=0, keepdims=True), 0.0)
                + jnp.where(row == rows - 1, jnp.sum(carry[4 + c], axis=0, keepdims=True), 0.0)
                + jnp.where((lane == 0) | (lane == lanes - 1), edge, 0.0)
            )
        return outs

    for k in range(ITERS):
        final = k == ITERS - 1
        sums = apply_operator(k)
        coarse = finish_coarse(k)
        corr = [coarse[c * per : c * per + rows, 0:lanes] for c in range(4)]
        apart = [[], [], [], []]
        for c in range(4):
            line = c * per + rows
            beside = coarse[c * per : c * per + rows, lanes : 2 * lanes]
            shifted = (
                jnp.where(row == 0, coarse[line : line + 1, 0:lanes], pltpu.roll(corr[c], 1, 0)),
                jnp.where(
                    row == rows - 1,
                    coarse[line + 1 : line + 2, 0:lanes],
                    pltpu.roll(corr[c], rows - 1, 0),
                ),
                jnp.where(lane == 0, beside, pltpu.roll(corr[c], 1, 1)),
                jnp.where(
                    lane == lanes - 1,
                    pltpu.roll(beside, lanes - 2, 1),
                    pltpu.roll(corr[c], lanes - 1, 1),
                ),
            )
            for n in range(4):
                apart[n].append(corr[c] - shifted[n])
        push = [lossy(apart[n]) for n in range(4)]
        push.append([mass[c % 2] * corr[c] for c in range(4)])
        ends = []
        for sign, weight in ((-1.0, wt[0]), (1.0, wt[ct])):
            over = turn(trig, corr, sign)
            ends.append([weight * x for x in lossy([corr[c] - over[c] for c in range(4)])])
        sums = fix_faces(k, sums)
        if not final:
            restrict_and_send(
                k + 1,
                [
                    sums[c] - coarse_change(moved, push, c) - ends[0][c] - ends[1][c]
                    for c in range(4)
                ],
            )
        for c in range(4):
            val_ref[c // 2, c % 2, 0] = val_ref[c // 2, c % 2, 0] - ends[0][c]
            val_ref[c // 2, c % 2, ct - 1] = val_ref[c // 2, c % 2, ct - 1] - ends[1][c]
        if final:
            for c in range(4):
                corr_ref[c] = corr[c]
                for n in range(5):
                    push_ref[n, c] = push[n][c]
            break

        on_faces(lambda d: halo_done(k, d, ha_send))

        def update_chunk(chunk, nothing):
            packed = zero
            for u in range(CHUNK):
                t = chunk * CHUNK + u
                weights = (wr_up[t], wr_dn[t], wa_lo[t], wa_hi[t], dens[t])
                res = [
                    (val_ref[c // 2, c % 2, t] - coarse_change(weights, push, c))
                    + face_terms(fix_rows, fix_cols, t, chunk, c, u)
                    for c in range(4)
                ]
                x = load(t)
                y = [None] * 4
                for h in range(2):
                    a, b = smooth(t, res[h], res[2 + h], h)
                    y[h], y[2 + h] = (x[h] + corr[h]) + a, (x[2 + h] + corr[2 + h]) + b
                for c in range(4):
                    sol_ref[c // 2, c % 2, t] = y[c]
                    packed = pack(y[c], c * CHUNK + u, packed)
            col_s[k + 1, chunk] = packed
            return nothing

        in_parts(k + 1, update_chunk, 0)

    on_faces(lambda d: stiff_copy(d).wait_send())

    on_faces(lambda d: halo_done(ITERS - 1, d, ha_send))

    for k in range(ITERS):
        gathered(k, ga_send)


def last_pass(
    sol_ref,
    val_ref,
    wr_up,
    wr_dn,
    wa_lo,
    wa_hi,
    dens,
    corr_ref,
    push_ref,
    fix_rows,
    fix_cols,
    sol_hbm,
    res_hbm,
    sol_out,
    res_out,
    sem,
):
    ct = sol_ref.shape[2]
    chunks = ct // CHUNK
    corr = [corr_ref[c] for c in range(4)]
    push = [[push_ref[n, c] for c in range(4)] for n in range(5)]

    def put(n, chunk):
        src, dst = ((sol_out, sol_hbm), (res_out, res_hbm))[n]
        at = pl.ds(chunk * CHUNK, CHUNK)
        return pltpu.make_async_copy(src.at[:, :, at], dst.at[:, :, at], sem.at[n, chunk])

    @pl.loop(0, chunks)
    def _(chunk):
        for u in range(CHUNK):
            t = chunk * CHUNK + u
            weights = (wr_up[t], wr_dn[t], wa_lo[t], wa_hi[t], dens[t])
            for c in range(4):
                sol_out[c // 2, c % 2, t] = sol_ref[c // 2, c % 2, t] + corr[c]
                res_out[c // 2, c % 2, t] = (
                    val_ref[c // 2, c % 2, t] - coarse_change(weights, push, c)
                ) + face_terms(fix_rows, fix_cols, t, chunk, c, u)
        for n in range(2):
            put(n, chunk).start()

    @pl.loop(0, chunks)
    def _(chunk):
        for n in range(2):
            put(n, chunk).wait()


def local(rhs, mat_ids, stiff_table, dens_table, mass_shift, harmonic, radial_factor, axial_factor):
    nrad = lax.axis_size("radial")
    nax = lax.axis_size("axial")
    ct, rows, lanes = mat_ids.shape
    vmem = pl.BlockSpec(memory_space=pltpu.VMEM)
    hbm = pl.BlockSpec(memory_space=pltpu.HBM)
    f32 = jnp.float32
    field = (ct, rows, lanes)
    chunks = ct // CHUNK
    groups = ct // GROUP
    cdev = 4 * (rows // AR)
    ndev = nrad * nax
    dma = pltpu.SemaphoreType.DMA
    inputs = (
        rhs,
        mat_ids,
        stiff_table,
        dens_table,
        mass_shift,
        harmonic,
        radial_factor,
        axial_factor,
    )
    held = (
        rhs.shape,
        rhs.shape,
        field,
        field,
        field,
        field,
        field,
        (4, rows, lanes),
        (5, 4, rows, lanes),
        (2, 4, ct, lanes),
        (chunks, rows, lanes),
    )
    state = pl.pallas_call(
        functools.partial(kernel, nrad, nax),
        out_shape=tuple(pltpu.VMEM(shape, f32) for shape in held),
        in_specs=[hbm] * 8,
        out_specs=(vmem,) * len(held),
        scratch_shapes=[
            pltpu.VMEM(rhs.shape, f32),
            pltpu.VMEM(field, jnp.int32),
            pltpu.SMEM(stiff_table.shape, f32),
            pltpu.SMEM(dens_table.shape, f32),
            pltpu.SMEM(mass_shift.shape, f32),
            pltpu.SMEM(harmonic.shape, jnp.int32),
            pltpu.VMEM(radial_factor.shape, f32),
            pltpu.VMEM(axial_factor.shape, f32),
            dma((8,)),
            pltpu.VMEM((ct + 2, rows, lanes), f32),
            pltpu.VMEM((ct + 1, rows, lanes), f32),
            pltpu.VMEM((2,) + field, f32),
            pltpu.VMEM(field, f32),
            pltpu.VMEM((2,) + field, f32),
            pltpu.VMEM((2, ct, lanes), f32),
            pltpu.VMEM((chunks, rows, lanes), f32),
            pltpu.VMEM((2, ct, lanes), f32),
            pltpu.VMEM((2, ct, lanes), f32),
            pltpu.VMEM((groups, rows, lanes), f32),
            pltpu.VMEM((2, groups, rows, lanes), f32),
            pltpu.VMEM((chunks, rows, lanes), f32),
            pltpu.VMEM((ITERS, 2, 2, 2, ct, lanes), f32),
            pltpu.VMEM((ITERS, chunks, rows, lanes), f32),
            pltpu.VMEM((ITERS, 2, chunks, rows, lanes), f32),
            pltpu.VMEM((ITERS, ndev, 1, lanes), f32),
            pltpu.VMEM((2, 3 * lanes, 3 * lanes), jnp.bfloat16),
            pltpu.VMEM((8 * rows, 6 * nrad * cdev), jnp.bfloat16),
            dma((4,)),
            dma((4,)),
            dma((ITERS, 4)),
            dma((ITERS, 4)),
            dma((ITERS,)),
            dma((ITERS,)),
        ],
        compiler_params=pltpu.CompilerParams(
            collective_id=0, has_side_effects=True, vmem_limit_bytes=48 * 1024 * 1024
        ),
    )(*[pltpu.with_memory_space_constraint(x, pltpu.HBM) for x in inputs])
    return pl.pallas_call(
        last_pass,
        out_shape=(jax.ShapeDtypeStruct(rhs.shape, f32), jax.ShapeDtypeStruct(rhs.shape, f32)),
        in_specs=[vmem] * len(held),
        out_specs=(hbm, hbm),
        scratch_shapes=[
            pltpu.VMEM(rhs.shape, f32),
            pltpu.VMEM(rhs.shape, f32),
            dma((2, chunks)),
        ],
        compiler_params=pltpu.CompilerParams(vmem_limit_bytes=32 * 1024 * 1024),
    )(*[pltpu.with_memory_space_constraint(x, pltpu.VMEM) for x in state])


def solution(mesh):
    return jax.shard_map(
        local,
        mesh=mesh,
        in_specs=(
            P(None, None, None, "radial", "axial"),
            P(None, "radial", "axial"),
            P(),
            P(),
            P(),
            P(),
            P(),
            P(),
        ),
        out_specs=(P(None, None, None, "radial", "axial"), P(None, None, None, "radial", "axial")),
        check_vma=False,
    )
```

```python
import functools

import jax
import jax.numpy as jnp
from jax import lax
from jax.experimental import pallas as pl
from jax.experimental.pallas import tpu as pltpu
from jax.sharding import PartitionSpec as P

ITERS = 3
NSECT = 24
AR = 4
AA = 8
LOSS_FACTOR = 0.2
RELAXATION = 0.6
MESH = pl.DeviceIdType.MESH
HIGHEST = lax.Precision.HIGHEST
CHUNK = 8
PARTS = 6
GROUP = 32


def dot(a, b):
    return jnp.dot(a, b, precision=HIGHEST, preferred_element_type=jnp.float32)


def dot16(a, b):
    return jnp.dot(a, b, preferred_element_type=jnp.float32)


def split(x):
    high = x.astype(jnp.bfloat16)
    return high, (x - high.astype(jnp.float32)).astype(jnp.bfloat16)


def left_parts(x):
    high, low = split(x)
    return jnp.concatenate([high, low, high], axis=1)


def right_parts(x, axis):
    high, low = split(x)
    return jnp.concatenate([high, high, low], axis=axis)


def grid_of(rows, lanes):
    return (
        lax.broadcasted_iota(jnp.int32, (rows, lanes), 0),
        lax.broadcasted_iota(jnp.int32, (rows, lanes), 1),
    )


def around(value, up, dn, edge):
    rows, lanes = value.shape
    row, lane = grid_of(rows, lanes)
    return (
        jnp.where(row == 0, up, pltpu.roll(value, 1, 0)),
        jnp.where(row == rows - 1, dn, pltpu.roll(value, rows - 1, 0)),
        pltpu.roll(jnp.where(lane == lanes - 1, edge, value), 1, 1),
        pltpu.roll(jnp.where(lane == 0, edge, value), lanes - 1, 1),
    )


def face_terms(fix_rows, fix_cols, t, chunk, c, u):
    rows, lanes = fix_cols.shape[1:]
    row, lane = grid_of(rows, lanes)
    edge = pltpu.roll(fix_cols[chunk], lanes - 1 - 2 * (c * CHUNK + u), 1)
    along = jnp.where(
        row == 0,
        fix_rows[0, c, pl.ds(t, 1), :],
        jnp.where(row == rows - 1, fix_rows[1, c, pl.ds(t, 1), :], 0.0),
    )
    return along + jnp.where((lane == 0) | (lane == lanes - 1), edge, 0.0)


def lossy(x):
    return [x[h] - LOSS_FACTOR * x[2 + h] for h in range(2)] + [
        x[2 + h] + LOSS_FACTOR * x[h] for h in range(2)
    ]


def coarse_change(weights, push, c):
    w_up, w_dn, w_lo, w_hi, dens = weights
    return ((w_up * push[0][c] + w_dn * push[1][c]) + (w_lo * push[2][c] + w_hi * push[3][c])) - (
        dens * push[4][c]
    )


def turn(trig, x, sign):
    cosines, sines = trig[0:2], trig[2:4]
    return [cosines[h] * x[h] - sign * sines[h] * x[2 + h] for h in range(2)] + [
        sign * sines[h] * x[h] + cosines[h] * x[2 + h] for h in range(2)
    ]


def kernel(
    nrad,
    nax,
    rhs_hbm,
    ids_hbm,
    stiff_hbm,
    dens_hbm,
    mass_hbm,
    harm_hbm,
    radial_hbm,
    axial_hbm,
    sol_ref,
    val_ref,
    wr_up,
    wr_dn,
    wa_lo,
    wa_hi,
    dens,
    corr_ref,
    push_ref,
    fix_rows,
    fix_cols,
    rhs_ref,
    ids_ref,
    stiff_ref,
    dens_ref,
    mass_ref,
    harm_ref,
    radial_ref,
    axial_ref,
    in_sem,
    stiff,
    wt,
    dr,
    di,
    sc,
    w_rows,
    w_cols,
    srow_s,
    srow_r,
    scol_s,
    scol_r,
    scol_m,
    row_r,
    col_s,
    col_r,
    all_r,
    axmat,
    radmat,
    st_send,
    st_recv,
    ha_send,
    ha_recv,
    ga_send,
    ga_recv,
):
    loads = [
        pltpu.make_async_copy(src, dst, in_sem.at[n])
        for n, (src, dst) in enumerate(
            (
                (stiff_hbm, stiff_ref),
                (ids_hbm, ids_ref),
                (rhs_hbm, rhs_ref),
                (dens_hbm, dens_ref),
                (mass_hbm, mass_ref),
                (harm_hbm, harm_ref),
                (radial_hbm, radial_ref),
                (axial_hbm, axial_ref),
            )
        )
    ]
    for load_in in loads:
        load_in.start()
    ct = rhs_ref.shape[2]
    rows, lanes = rhs_ref.shape[3:]
    gr = radial_ref.shape[2]
    ga = axial_ref.shape[2]
    band_r = rows // AR
    band_c = lanes // AA
    chunks = ct // CHUNK
    ndev = nrad * nax
    i = lax.axis_index("radial")
    j = lax.axis_index("axial")
    me = i * nax + j
    has_up, has_dn = i > 0, i < nrad - 1
    has_lo, has_hi = j > 0, j < nax - 1
    conds = (has_up, has_dn, has_lo, has_hi)
    targets = ({"radial": i - 1}, {"radial": i + 1}, {"axial": j - 1}, {"axial": j + 1})

    def each_peer(act):
        def along(a):
            to = i + a
            to = jnp.where(to >= nrad, to - nrad, to)
            for b in range(nax):
                at = j + b
                act({"radial": to, "axial": jnp.where(at >= nax, at - nax, at)})

        for b in range(1, nax):
            at = j + b
            act({"radial": i, "axial": jnp.where(at >= nax, at - nax, at)})
        if nrad <= 8:
            for a in range(1, nrad):
                along(a)
        else:
            pl.loop(1, nrad)(along)

    barrier = pltpu.get_barrier_semaphore()
    each_peer(
        lambda peer: pl.semaphore_signal(barrier, inc=1, device_id=peer, device_id_type=MESH)
    )

    for d in range(4):

        @pl.when(jnp.logical_not(conds[d]))
        def _():
            if d < 2:
                srow_r[d] = jnp.zeros(srow_r.shape[1:], jnp.float32)
                for k in range(ITERS):
                    row_r[k, d] = jnp.zeros(row_r.shape[2:], jnp.float32)
            else:
                scol_r[d - 2] = jnp.zeros(scol_r.shape[1:], jnp.float32)
                for k in range(ITERS):
                    col_r[k, d - 2] = jnp.zeros(col_r.shape[2:], jnp.float32)

    row, lane = grid_of(rows, lanes)
    zero = jnp.zeros((rows, lanes), jnp.float32)
    pair = lane // 2
    odd_lane = lane % 2 == 1

    def lookup(ids, table):
        value = jnp.full(ids.shape, table[0], jnp.float32)
        for entry in range(1, table.shape[0]):
            value = jnp.where(ids == entry, table[entry], value)
        return value

    def pack(value, at, packed):
        return jnp.where(pair == at, pltpu.roll(value, (2 * at + 1) % lanes, 1), packed)

    def stiff_copy(d):
        if d < 2:
            src, dst = srow_s.at[d], srow_r.at[1 - d]
        else:
            src, dst = scol_s, scol_r.at[3 - d]
        return pltpu.make_async_remote_copy(
            src_ref=src,
            dst_ref=dst,
            send_sem=st_send.at[d],
            recv_sem=st_recv.at[d ^ 1],
            device_id=targets[d],
            device_id_type=MESH,
        )

    part_chunks = chunks // PARTS
    part_ct = ct // PARTS

    def halo_copy(k, part, d):
        if d < 2:
            at = pl.ds(part * part_ct, part_ct)
            line = 0 if d == 0 else rows - 1
            src, dst = sol_ref.at[:, :, at, line], row_r.at[k, 1 - d, :, :, at]
        else:
            at = pl.ds(part * part_chunks, part_chunks)
            src, dst = col_s.at[k, at], col_r.at[k, 3 - d, at]
        return pltpu.make_async_remote_copy(
            src_ref=src,
            dst_ref=dst,
            send_sem=ha_send.at[k, d],
            recv_sem=ha_recv.at[k, d ^ 1],
            device_id=targets[d],
            device_id_type=MESH,
        )

    def halo_done(k, d, sem):
        got = row_r.at[k, d] if d < 2 else col_r.at[k, d - 2]
        pltpu.make_async_copy(got, got, sem.at[k, d]).wait()

    def gather(k, peer):
        return pltpu.make_async_remote_copy(
            src_ref=all_r.at[k, me],
            dst_ref=all_r.at[k, me],
            send_sem=ga_send.at[k],
            recv_sem=ga_recv.at[k],
            device_id=peer,
            device_id_type=MESH,
        )

    def gathered(k, sem):
        others = all_r.at[k, pl.ds(1, ndev - 1)]
        pltpu.make_async_copy(others, others, sem.at[k]).wait()

    def on_faces(act):
        for d in range(4):

            @pl.when(conds[d])
            def _():
                act(d)

    loads[0].wait()
    loads[1].wait()

    @pl.loop(0, ct // GROUP)
    def _(group):
        packed = zero
        for u in range(GROUP):
            t = group * GROUP + u
            value = lookup(ids_ref[t], stiff_ref)
            stiff[t + 1] = value
            srow_s[0, pl.ds(t, 1), :] = value[0:1]
            srow_s[1, pl.ds(t, 1), :] = value[rows - 1 : rows]
            packed = pack(value, u, packed)
        scol_s[group] = packed

    stiff[0] = stiff[ct]
    stiff[ct + 1] = stiff[1]

    pl.semaphore_wait(barrier, ndev - 1)
    on_faces(lambda d: stiff_copy(d).start())

    e_row, e_col = grid_of(lanes, lanes)
    fold = jnp.where(e_row // AA == e_col % band_c, 1.0, 0.0).astype(jnp.bfloat16)
    fold = jnp.concatenate([fold, fold], axis=0)
    k_row, k_col = grid_of(4 * rows, lanes)
    keep = k_row // AR == (j + rows - k_col // band_c) % rows

    def restrict_and_send(k, sums):
        folded = dot16(jnp.concatenate(split(jnp.concatenate(sums, axis=0)), axis=1), fold)
        all_r[k, me] = jnp.sum(jnp.where(keep, folded, 0.0), axis=0, keepdims=True)
        each_peer(lambda peer: gather(k, peer).start())

    loads[2].wait()

    def sum_pass(chunk, sums):
        sums = list(sums)
        for u in range(CHUNK):
            for c in range(4):
                sums[c] = sums[c] + rhs_ref[c // 2, c % 2, chunk * CHUNK + u]
        return tuple(sums)

    restrict_and_send(0, lax.fori_loop(0, chunks, sum_pass, (zero,) * 4))
    for load_in in loads[3:]:
        load_in.wait()

    ax_row, ax_col = grid_of(lanes, ga)
    own = jnp.where(ax_row // AA + j * band_c == ax_col, 1.0, 0.0)
    half = lanes // 2
    side = jnp.where(ax_row % 2 == 0, j * band_c - 1, (j + 1) * band_c) == ax_col
    edges = [jnp.where(side & (ax_row // half == p), 1.0, 0.0) for p in range(2)]
    spare = [jnp.zeros((3 * lanes, lanes - ga), jnp.float32)] if ga < lanes else []
    for h in range(2):
        wide = jnp.concatenate(
            [
                dot(own, axial_ref[0, h]),
                dot(own, axial_ref[1, h]),
                dot(edges[0], axial_ref[0, h]) + dot(edges[1], axial_ref[1, h]),
            ],
            axis=0,
        )
        axmat[h] = right_parts(jnp.concatenate([wide] + spare, axis=1), 1)

    per = 2 * rows
    cdev = 4 * band_r
    r_row, r_col = grid_of(4 * per, gr)
    r_row = r_row % per
    want = jnp.where(
        r_row < rows,
        r_row // AR + i * band_r,
        jnp.where(
            r_row == rows, i * band_r - 1, jnp.where(r_row == rows + 1, (i + 1) * band_r, -1)
        ),
    )
    r_sel = jnp.where(want == r_col, 1.0, 0.0)
    c_row, c_col = grid_of(gr, nrad * cdev)
    c_sel = jnp.where((c_col // cdev) * band_r + c_col % band_r == c_row, 1.0, 0.0)
    m_row, m_col = grid_of(4 * per, nrad * cdev)
    m_out = m_row // per
    m_in = (m_col % cdev) // band_r
    first = jnp.zeros((4 * per, nrad * cdev), jnp.float32)
    second = first
    for h in range(2):
        same = (m_out == m_in) & (m_out % 2 == h)
        to_re = (m_out == h) & (m_in == 2 + h)
        to_im = (m_out == 2 + h) & (m_in == h)
        real = dot(dot(r_sel, radial_ref[0, h]), c_sel)
        imag = dot(dot(r_sel, radial_ref[1, h]), c_sel)
        first = jnp.where(same, real, first)
        first = jnp.where(to_re, -imag, first)
        first = jnp.where(to_im, imag, first)
        second = jnp.where(same, -imag, second)
        second = jnp.where(to_re, -real, second)
        second = jnp.where(to_im, real, second)
    radmat[...] = left_parts(jnp.concatenate([first, second], axis=1))

    p_row, _ = grid_of(nrad * cdev, 3 * lanes)
    odd_harm = (p_row // band_r) % 2 == 1

    def finish_coarse(k):
        gathered(k, ga_recv)

        tiles = []
        for a in range(nrad):
            tile = zero
            for b in range(nax):
                tile = jnp.where((lane // band_c + row) % rows == b, all_r[k, a * nax + b], tile)
            tile = pltpu.roll(tile, 0, 1, stride=band_c, stride_axis=0)
            tiles.append(tile)
        whole = left_parts(jnp.concatenate(tiles, axis=0))
        prod = [
            lax.dot_general(
                whole,
                axmat[h],
                (((1,), (1,)), ((), ())),
                preferred_element_type=jnp.float32,
            )
            for h in range(2)
        ]
        prod = jnp.where(odd_harm, prod[1], prod[0])
        a = prod[:, 0:lanes]
        b = prod[:, lanes : 2 * lanes]
        e = prod[:, 2 * lanes : 3 * lanes]
        f = pltpu.roll(e, half, 1)
        mixed = jnp.concatenate(
            [jnp.concatenate([a, e], axis=1), jnp.concatenate([b, f], axis=1)], axis=0
        )
        return dot16(radmat[...], right_parts(mixed, 0))

    trig = [[], []]
    for h in range(2):
        angle = jnp.full((rows, lanes), harm_ref[h], jnp.int32).astype(jnp.float32) * (
            2.0 * jnp.pi / NSECT
        )
        trig[0].append(jnp.cos(angle))
        trig[1].append(jnp.sin(angle))
    trig = trig[0] + trig[1]

    on_faces(lambda d: stiff_copy(d ^ 1).wait_recv())

    mass = [mass_ref[0], mass_ref[1]]

    def smooth(t, rr, ri, h):
        d_re, d_im, scale = dr[h, t], di[t], sc[h, t]
        return (d_re * rr + d_im * ri) * scale, (d_re * ri - d_im * rr) * scale

    per_group = GROUP // CHUNK
    for n in range(ct // GROUP):
        merged = jnp.where(odd_lane, scol_r[1, n], scol_r[0, n])
        for m in range(per_group):
            scol_m[n * per_group + m] = (
                merged if m == 0 else pltpu.roll(merged, lanes - 2 * CHUNK * m, 1)
            )

    def setup_step(t, u, packed, faces, beside, moved):
        value = stiff[t + 1]
        up, dn, lo, hi = around(
            value,
            srow_r[0, pl.ds(t, 1), :],
            srow_r[1, pl.ds(t, 1), :],
            pltpu.roll(beside, lanes - 1 - 2 * u, 1),
        )
        c_up, c_dn = 0.5 * (value + up), 0.5 * (value + dn)
        c_lo, c_hi = 0.5 * (value + lo), 0.5 * (value + hi)
        c_be, c_ah = 0.5 * (value + stiff[t]), 0.5 * (value + stiff[t + 2])
        wr_up[t] = c_up
        wr_dn[t] = c_dn
        wa_lo[t] = c_lo
        wa_hi[t] = c_hi
        w_rows[0, pl.ds(t, 1), :] = c_up[0:1]
        w_rows[1, pl.ds(t, 1), :] = c_dn[rows - 1 : rows]
        wt[t] = c_be
        wt[t + 1] = c_ah
        total = c_dn + c_up + c_hi + c_lo + c_ah + c_be
        density = lookup(ids_ref[t], dens_ref)
        dens[t] = density
        moved = [m + w for m, w in zip(moved, (c_up, c_dn, c_lo, c_hi, density))]
        d_im = LOSS_FACTOR * total
        di[t] = d_im
        y = [None] * 4
        for h in range(2):
            d_re = total - mass[h] * density
            scale = RELAXATION / (d_re * d_re + d_im * d_im)
            dr[h, t] = d_re
            sc[h, t] = scale
            rr, ri = rhs_ref[0, h, t], rhs_ref[1, h, t]
            y[h] = (d_re * rr + d_im * ri) * scale
            y[2 + h] = (d_re * ri - d_im * rr) * scale
            sol_ref[0, h, t] = y[h]
            sol_ref[1, h, t] = y[2 + h]
        for c in range(4):
            packed = pack(y[c], c * CHUNK + u, packed)
        faces = pack(jnp.where(lane == 0, c_lo, c_hi), u, faces)
        return packed, faces, moved

    def in_parts(k, step, carry):
        def one_part(part, carry):
            carry = lax.fori_loop(
                0,
                part_chunks,
                lambda n, carry: step(part * part_chunks + n, carry),
                carry,
                unroll=True,
            )
            on_faces(lambda d: halo_copy(k, part, d).start())
            return carry

        return lax.fori_loop(0, PARTS, one_part, carry)

    def setup_chunk(chunk, moved):
        packed = zero
        faces = zero
        beside = scol_m[chunk]
        for u in range(CHUNK):
            packed, faces, moved = setup_step(chunk * CHUNK + u, u, packed, faces, beside, moved)
        col_s[0, chunk] = packed
        faces = faces + pltpu.roll(faces, 2 * CHUNK, 1)
        w_cols[chunk] = faces + pltpu.roll(faces, 4 * CHUNK, 1)
        return tuple(moved)

    moved = in_parts(0, setup_chunk, (zero,) * 5)


    def load(t):
        return [sol_ref[c // 2, c % 2, t] for c in range(4)]

    def apply_operator(k):
        start = load(0)
        beyond = turn(trig, start, 1.0)
        before = turn(trig, load(ct - 1), -1.0)

        def chunk_pass(chunk, carry):
            xm, x, sums = list(carry[0:4]), list(carry[4:8]), list(carry[8:])
            for u in range(CHUNK):
                t = chunk * CHUNK + u
                if u < CHUNK - 1:
                    xp = load(t + 1)
                else:
                    ended = t == ct - 1
                    xp = load(jnp.minimum(t + 1, ct - 1))
                    xp = [jnp.where(ended, beyond[c], xp[c]) for c in range(4)]
                c_up, c_dn, c_lo, c_hi = wr_up[t], wr_dn[t], wa_lo[t], wa_hi[t]
                c_be, c_ah = wt[t], wt[t + 1]
                nb = []
                for c in range(4):
                    up = jnp.where(row == 0, 0.0, pltpu.roll(x[c], 1, 0))
                    dn = jnp.where(row == rows - 1, 0.0, pltpu.roll(x[c], rows - 1, 0))
                    lo = jnp.where(lane == 0, 0.0, pltpu.roll(x[c], 1, 1))
                    hi = jnp.where(lane == lanes - 1, 0.0, pltpu.roll(x[c], lanes - 1, 1))
                    nb.append(
                        (c_dn * dn + c_up * up)
                        + (c_hi * hi + c_lo * lo)
                        + (c_ah * xp[c] + c_be * xm[c])
                    )
                nb = lossy(nb)
                d_im = di[t]
                for h in range(2):
                    d_re = dr[h, t]
                    re, im = h, 2 + h
                    val_re = rhs_ref[0, h, t] - (d_re * x[re] - d_im * x[im] - nb[re])
                    val_im = rhs_ref[1, h, t] - (d_re * x[im] + d_im * x[re] - nb[im])
                    val_ref[0, h, t] = val_re
                    val_ref[1, h, t] = val_im
                    sums[re] = sums[re] + val_re
                    sums[im] = sums[im] + val_im
                xm, x = x, xp
            return tuple(xm) + tuple(x) + tuple(sums)

        carry = tuple(before) + tuple(start) + (zero,) * 4
        return lax.fori_loop(0, chunks, chunk_pass, carry, unroll=3)[8:]

    def fix_faces(k, sums):
        on_faces(lambda d: halo_done(k, d, ha_recv))

        def chunk_fix(chunk, carry):
            out = []
            at = pl.ds(pl.multiple_of(chunk * CHUNK, CHUNK), CHUNK)
            for side in range(2):
                weight = w_rows[side, at]
                term = lossy([weight * row_r[k, side, c // 2, c % 2, at] for c in range(4)])
                for c in range(4):
                    fix_rows[side, c, at] = term[c]
                    out.append(carry[4 * side + c] + term[c])
            term = w_cols[chunk] * jnp.where(
                odd_lane,
                pltpu.roll(col_r[k, 0, chunk], 1, 1),
                pltpu.roll(col_r[k, 1, chunk], lanes - 1, 1),
            )
            turned = jnp.where(
                pair < 2 * CHUNK,
                -pltpu.roll(term, lanes - 4 * CHUNK, 1),
                pltpu.roll(term, 4 * CHUNK, 1),
            )
            term = term + LOSS_FACTOR * turned
            fix_cols[chunk] = term
            return tuple(out) + (carry[8] + term,)

        carry = lax.fori_loop(0, chunks, chunk_fix, (zero,) * 9, unroll=12)
        beside = carry[8]
        step = 1
        while step < CHUNK:
            beside = beside + pltpu.roll(beside, lanes - 2 * step, 1)
            step *= 2
        outs = []
        for c in range(4):
            edge = pltpu.roll(beside, lanes - 1 - 2 * c * CHUNK, 1)
            outs.append(
                sums[c]
                + jnp.where(row == 0, jnp.sum(carry[c], axis=0, keepdims=True), 0.0)
                + jnp.where(row == rows - 1, jnp.sum(carry[4 + c], axis=0, keepdims=True), 0.0)
                + jnp.where((lane == 0) | (lane == lanes - 1), edge, 0.0)
            )
        return outs

    for k in range(ITERS):
        final = k == ITERS - 1
        sums = apply_operator(k)
        coarse = finish_coarse(k)
        corr = [coarse[c * per : c * per + rows, 0:lanes] for c in range(4)]
        apart = [[], [], [], []]
        for c in range(4):
            line = c * per + rows
            beside = coarse[c * per : c * per + rows, lanes : 2 * lanes]
            shifted = (
                jnp.where(row == 0, coarse[line : line + 1, 0:lanes], pltpu.roll(corr[c], 1, 0)),
                jnp.where(
                    row == rows - 1,
                    coarse[line + 1 : line + 2, 0:lanes],
                    pltpu.roll(corr[c], rows - 1, 0),
                ),
                jnp.where(lane == 0, beside, pltpu.roll(corr[c], 1, 1)),
                jnp.where(
                    lane == lanes - 1,
                    pltpu.roll(beside, lanes - 2, 1),
                    pltpu.roll(corr[c], lanes - 1, 1),
                ),
            )
            for n in range(4):
                apart[n].append(corr[c] - shifted[n])
        push = [lossy(apart[n]) for n in range(4)]
        push.append([mass[c % 2] * corr[c] for c in range(4)])
        ends = []
        for sign, weight in ((-1.0, wt[0]), (1.0, wt[ct])):
            over = turn(trig, corr, sign)
            ends.append([weight * x for x in lossy([corr[c] - over[c] for c in range(4)])])
        sums = fix_faces(k, sums)
        if not final:
            restrict_and_send(
                k + 1,
                [
                    sums[c] - coarse_change(moved, push, c) - ends[0][c] - ends[1][c]
                    for c in range(4)
                ],
            )
        for c in range(4):
            val_ref[c // 2, c % 2, 0] = val_ref[c // 2, c % 2, 0] - ends[0][c]
            val_ref[c // 2, c % 2, ct - 1] = val_ref[c // 2, c % 2, ct - 1] - ends[1][c]
        if final:
            for c in range(4):
                corr_ref[c] = corr[c]
                for n in range(5):
                    push_ref[n, c] = push[n][c]
            break

        on_faces(lambda d: halo_done(k, d, ha_send))

        def update_chunk(chunk, nothing):
            packed = zero
            for u in range(CHUNK):
                t = chunk * CHUNK + u
                weights = (wr_up[t], wr_dn[t], wa_lo[t], wa_hi[t], dens[t])
                res = [
                    (val_ref[c // 2, c % 2, t] - coarse_change(weights, push, c))
                    + face_terms(fix_rows, fix_cols, t, chunk, c, u)
                    for c in range(4)
                ]
                x = load(t)
                y = [None] * 4
                for h in range(2):
                    a, b = smooth(t, res[h], res[2 + h], h)
                    y[h], y[2 + h] = (x[h] + corr[h]) + a, (x[2 + h] + corr[2 + h]) + b
                for c in range(4):
                    sol_ref[c // 2, c % 2, t] = y[c]
                    packed = pack(y[c], c * CHUNK + u, packed)
            col_s[k + 1, chunk] = packed
            return nothing

        in_parts(k + 1, update_chunk, 0)

    on_faces(lambda d: stiff_copy(d).wait_send())

    on_faces(lambda d: halo_done(ITERS - 1, d, ha_send))

    for k in range(ITERS):
        gathered(k, ga_send)


def last_pass(
    sol_ref,
    val_ref,
    wr_up,
    wr_dn,
    wa_lo,
    wa_hi,
    dens,
    corr_ref,
    push_ref,
    fix_rows,
    fix_cols,
    sol_hbm,
    res_hbm,
    sol_out,
    res_out,
    sem,
):
    ct = sol_ref.shape[2]
    chunks = ct // CHUNK
    corr = [corr_ref[c] for c in range(4)]
    push = [[push_ref[n, c] for c in range(4)] for n in range(5)]

    def put(n, chunk):
        src, dst = ((sol_out, sol_hbm), (res_out, res_hbm))[n]
        at = pl.ds(chunk * CHUNK, CHUNK)
        return pltpu.make_async_copy(src.at[:, :, at], dst.at[:, :, at], sem.at[n, chunk])

    @pl.loop(0, chunks, unroll=3)
    def _(chunk):
        for u in range(CHUNK):
            t = chunk * CHUNK + u
            weights = (wr_up[t], wr_dn[t], wa_lo[t], wa_hi[t], dens[t])
            for c in range(4):
                sol_out[c // 2, c % 2, t] = sol_ref[c // 2, c % 2, t] + corr[c]
                res_out[c // 2, c % 2, t] = (
                    val_ref[c // 2, c % 2, t] - coarse_change(weights, push, c)
                ) + face_terms(fix_rows, fix_cols, t, chunk, c, u)
        for n in range(2):
            put(n, chunk).start()

    @pl.loop(0, chunks)
    def _(chunk):
        for n in range(2):
            put(n, chunk).wait()


def local(rhs, mat_ids, stiff_table, dens_table, mass_shift, harmonic, radial_factor, axial_factor):
    nrad = lax.axis_size("radial")
    nax = lax.axis_size("axial")
    ct, rows, lanes = mat_ids.shape
    vmem = pl.BlockSpec(memory_space=pltpu.VMEM)
    hbm = pl.BlockSpec(memory_space=pltpu.HBM)
    f32 = jnp.float32
    field = (ct, rows, lanes)
    chunks = ct // CHUNK
    groups = ct // GROUP
    cdev = 4 * (rows // AR)
    ndev = nrad * nax
    dma = pltpu.SemaphoreType.DMA
    inputs = (
        rhs,
        mat_ids,
        stiff_table,
        dens_table,
        mass_shift,
        harmonic,
        radial_factor,
        axial_factor,
    )
    held = (
        rhs.shape,
        rhs.shape,
        field,
        field,
        field,
        field,
        field,
        (4, rows, lanes),
        (5, 4, rows, lanes),
        (2, 4, ct, lanes),
        (chunks, rows, lanes),
    )
    state = pl.pallas_call(
        functools.partial(kernel, nrad, nax),
        out_shape=tuple(pltpu.VMEM(shape, f32) for shape in held),
        in_specs=[hbm] * 8,
        out_specs=(vmem,) * len(held),
        scratch_shapes=[
            pltpu.VMEM(rhs.shape, f32),
            pltpu.VMEM(field, jnp.int32),
            pltpu.SMEM(stiff_table.shape, f32),
            pltpu.SMEM(dens_table.shape, f32),
            pltpu.SMEM(mass_shift.shape, f32),
            pltpu.SMEM(harmonic.shape, jnp.int32),
            pltpu.VMEM(radial_factor.shape, f32),
            pltpu.VMEM(axial_factor.shape, f32),
            dma((8,)),
            pltpu.VMEM((ct + 2, rows, lanes), f32),
            pltpu.VMEM((ct + 1, rows, lanes), f32),
            pltpu.VMEM((2,) + field, f32),
            pltpu.VMEM(field, f32),
            pltpu.VMEM((2,) + field, f32),
            pltpu.VMEM((2, ct, lanes), f32),
            pltpu.VMEM((chunks, rows, lanes), f32),
            pltpu.VMEM((2, ct, lanes), f32),
            pltpu.VMEM((2, ct, lanes), f32),
            pltpu.VMEM((groups, rows, lanes), f32),
            pltpu.VMEM((2, groups, rows, lanes), f32),
            pltpu.VMEM((chunks, rows, lanes), f32),
            pltpu.VMEM((ITERS, 2, 2, 2, ct, lanes), f32),
            pltpu.VMEM((ITERS, chunks, rows, lanes), f32),
            pltpu.VMEM((ITERS, 2, chunks, rows, lanes), f32),
            pltpu.VMEM((ITERS, ndev, 1, lanes), f32),
            pltpu.VMEM((2, 3 * lanes, 3 * lanes), jnp.bfloat16),
            pltpu.VMEM((8 * rows, 6 * nrad * cdev), jnp.bfloat16),
            dma((4,)),
            dma((4,)),
            dma((ITERS, 4)),
            dma((ITERS, 4)),
            dma((ITERS,)),
            dma((ITERS,)),
        ],
        compiler_params=pltpu.CompilerParams(
            collective_id=0, has_side_effects=True, vmem_limit_bytes=48 * 1024 * 1024
        ),
    )(*[pltpu.with_memory_space_constraint(x, pltpu.HBM) for x in inputs])
    return pl.pallas_call(
        last_pass,
        out_shape=(jax.ShapeDtypeStruct(rhs.shape, f32), jax.ShapeDtypeStruct(rhs.shape, f32)),
        in_specs=[vmem] * len(held),
        out_specs=(hbm, hbm),
        scratch_shapes=[
            pltpu.VMEM(rhs.shape, f32),
            pltpu.VMEM(rhs.shape, f32),
            dma((2, chunks)),
        ],
        compiler_params=pltpu.CompilerParams(vmem_limit_bytes=32 * 1024 * 1024),
    )(*[pltpu.with_memory_space_constraint(x, pltpu.VMEM) for x in state])


def solution(mesh):
    return jax.shard_map(
        local,
        mesh=mesh,
        in_specs=(
            P(None, None, None, "radial", "axial"),
            P(None, "radial", "axial"),
            P(),
            P(),
            P(),
            P(),
            P(),
            P(),
        ),
        out_specs=(P(None, None, None, "radial", "axial"), P(None, None, None, "radial", "axial")),
        check_vma=False,
    )
```
